32 devices in a mesh: pb: 8 (over y, x, core), ka: 4 (over z).
Axes of the slice: x: 2, y: 2, z: 4, core: 2. Of those that a mesh axis runs over, the one named last changes fastest.
Arguments:
- tokens: bfloat16 [32768, 768], P(('pb', 'ka')), may hold values from -6 to 6
- sequence_ids: int32 [32768], P(('pb', 'ka')), may hold values from 0 to 31, as said below
- sequence_offsets: int32 [32768], P(('pb', 'ka')), may hold values from 0 to 2047, as said below
- signed_norm_gain: bfloat16 [768], replicated, may hold values from 0.099609375 to 1.8984375
- signed_norm_bias: bfloat16 [768], replicated, may hold values from -1.75 to 1.75
- signed_query: bfloat16 [768, 768], replicated, may hold values from -0.21875 to 0.21875
- signed_key: bfloat16 [768, 768], replicated, may hold values from -0.21875 to 0.21875
- signed_value: bfloat16 [768, 768], replicated, may hold values from -0.21875 to 0.21875
- signed_out: bfloat16 [768, 768], replicated, may hold values from -1.75 to 1.75
- signed_mlp_gain: bfloat16 [768], replicated, may hold values from 0.099609375 to 1.8984375
- signed_mlp_bias: bfloat16 [768], replicated, may hold values from -1.75 to 1.75
- signed_up: bfloat16 [768, 3072], replicated, may hold values from -0.21875 to 0.21875
- signed_up_bias: bfloat16 [3072], replicated, may hold values from -3 to 3
- signed_down: bfloat16 [3072, 768], replicated, may hold values from -0.109375 to 0.109375
- signed_down_bias: bfloat16 [768], replicated, may hold values from -1.75 to 1.75
- plain_norm_gain: bfloat16 [768], replicated, may hold values from 0.099609375 to 1.8984375
- plain_norm_bias: bfloat16 [768], replicated, may hold values from -1.75 to 1.75
- plain_query: bfloat16 [768, 768], replicated, may hold values from -0.21875 to 0.21875
- plain_key: bfloat16 [768, 768], replicated, may hold values from -0.21875 to 0.21875
- plain_value: bfloat16 [768, 768], replicated, may hold values from -0.21875 to 0.21875
- plain_out: bfloat16 [768, 768], replicated, may hold values from -1.75 to 1.75
- plain_mlp_gain: bfloat16 [768], replicated, may hold values from 0.099609375 to 1.8984375
- plain_mlp_bias: bfloat16 [768], replicated, may hold values from -1.75 to 1.75
- plain_up: bfloat16 [768, 3072], replicated, may hold values from -0.21875 to 0.21875
- plain_up_bias: bfloat16 [3072], replicated, may hold values from -3 to 3
- plain_down: bfloat16 [3072, 768], replicated, may hold values from -0.109375 to 0.109375
- plain_down_bias: bfloat16 [768], replicated, may hold values from -1.75 to 1.75
- cotangent: bfloat16 [32768, 768], P(('pb', 'ka')), may hold values from -6 to 6
Outputs:
- output: bfloat16 [32768, 768], P(('pb', 'ka'))
- input_gradient: float32 [32768, 768], P(('pb', 'ka'))
- signed_norm_gain_gradient: float32 [768], replicated
- signed_norm_bias_gradient: float32 [768], replicated
- signed_query_gradient: float32 [768, 768], P('pb', 'ka')
- signed_key_gradient: float32 [768, 768], P('pb', 'ka')
- signed_value_gradient: float32 [768, 768], P('pb', 'ka')
- signed_out_gradient: float32 [768, 768], P('pb', 'ka')
- signed_mlp_gain_gradient: float32 [768], replicated
- signed_mlp_bias_gradient: float32 [768], replicated
- signed_up_gradient: float32 [768, 3072], P('pb', 'ka')
- signed_up_bias_gradient: float32 [3072], replicated
- signed_down_gradient: float32 [3072, 768], P('pb', 'ka')
- signed_down_bias_gradient: float32 [768], replicated
- plain_norm_gain_gradient: float32 [768], replicated
- plain_norm_bias_gradient: float32 [768], replicated
- plain_query_gradient: float32 [768, 768], P('pb', 'ka')
- plain_key_gradient: float32 [768, 768], P('pb', 'ka')
- plain_value_gradient: float32 [768, 768], P('pb', 'ka')
- plain_out_gradient: float32 [768, 768], P('pb', 'ka')
- plain_mlp_gain_gradient: float32 [768], replicated
- plain_mlp_bias_gradient: float32 [768], replicated
- plain_up_gradient: float32 [768, 3072], P('pb', 'ka')
- plain_up_bias_gradient: float32 [3072], replicated
- plain_down_gradient: float32 [3072, 768], P('pb', 'ka')
- plain_down_bias_gradient: float32 [768], replicated
The draws below stay inside these ranges and needn't reach their ends.
Inputs may be any that keep to these rules, and one draw needn't show every extreme that they name: `sequence_ids`: A sequence's tokens all lie in one group: rows b * 512 to (b + 1) * 512 - 1 of each device along ka at one index of pb, for one b below 2. A group holds one sequence of 2048 tokens or two of 1024; at half of the indices of pb every group holds two, at the other half one. Each half of a device's rows of a group belongs to one sequence, and every sequence has rows on every device along ka. `sequence_offsets`: the offsets of a sequence's tokens are 0 to its length minus 1, each once; within each half of a device's rows of a group they rise by one from row to row.
All inputs are finite; a program needn't handle non-finite values.
Results may differ from the reference program's by a relative error of at most 0.035.
Values may be sent and summed in bfloat16 or wider, within the bound.
No kernel may reach another device: no remote copies, remote signals or barrier semaphores. Data moves between devices by JAX's collectives and lax.ppermute only.
A program may use at most 704 MiB of HBM per device.

```python
import jax
import jax.numpy as jnp
from jax import lax

D = 768
HEADS = 12
HEAD_DIM = 64
FF = 3072
LONG = 2048
BATCH = 2
TOKENS = 32768
N_PB = 8
N_KA = 4


def sequence_layout(key):
    groups = N_PB * BATCH
    stretch = LONG // (2 * N_KA)
    row_rank = jax.random.permutation(jax.random.fold_in(key, 101), N_PB)
    short_kind = jnp.repeat(row_rank < N_PB // 2, BATCH)[:, None, None]
    long_keys = jax.random.split(jax.random.fold_in(key, 102), groups)
    long_piece = jax.vmap(lambda subkey: jax.random.permutation(subkey, 2 * N_KA))(long_keys).reshape(groups, N_KA, 2)
    short_keys = jax.random.split(jax.random.fold_in(key, 103), groups * 2)
    short_piece = jax.vmap(lambda subkey: jax.random.permutation(subkey, N_KA))(short_keys).reshape(groups, 2, N_KA)
    short_piece = jnp.transpose(short_piece, (0, 2, 1))
    piece_index = jnp.where(short_kind, short_piece, long_piece).astype(jnp.int32)
    offsets = piece_index[..., None] * stretch + jnp.arange(stretch, dtype=jnp.int32)
    group_number = jnp.arange(groups, dtype=jnp.int32)[:, None, None]
    slot_index = jnp.arange(2, dtype=jnp.int32)[None, None, :]
    labels = jnp.where(short_kind, 2 * group_number + slot_index, 2 * group_number + group_number % 2)
    labels = jnp.broadcast_to(labels[..., None], offsets.shape).astype(jnp.int32)

    def arrange(stacked):
        stacked = stacked.reshape(N_PB, BATCH, N_KA, 2, stretch)
        return jnp.transpose(stacked, (0, 2, 1, 3, 4)).reshape(N_PB * N_KA * BATCH * 2 * stretch)
    return (arrange(labels), arrange(offsets))


def draw_sequence_ids(key, part):
    shared = sequence_layout(key)
    return shared[0]


def draw_sequence_offsets(key, part):
    shared = sequence_layout(key)
    return shared[1]


def with_spikes(entries, stream_key, source, target, parts, factor):
    def block_of(position):
        return (jnp.arange(entries.shape[position]) // (entries.shape[position] // parts)).reshape((-1,) + (1,) * (entries.ndim - 1 - position))

    near = jax.random.permutation(stream_key, parts)[block_of(target)]
    second = (block_of(target) + parts // 2) % parts
    return jnp.where((block_of(source) == near) | (block_of(source) == second), factor * entries, entries)


def shard_levels(own_key, dims, shards, smallest, top_value):
    level, own = 1.0, jax.random.fold_in(own_key, 6)
    for position, parts in shards:
        steps = jnp.exp(jax.random.uniform(jax.random.fold_in(own, position), (parts,), jnp.float32, smallest / len(shards), top_value / len(shards)))
        level = level * jnp.repeat(steps, dims[position] // parts).reshape([-1 if axis == position else 1 for axis in range(len(dims))])
    return level


def centred(rng, shape, scale, limit, shards=(), kind=jnp.bfloat16):
    level = shard_levels(rng, shape, shards, -0.22, 0.18) if shards else 1.0
    array = jax.random.normal(rng, shape, jnp.float32) * scale * level
    return jnp.minimum(jnp.maximum(array, -limit), limit).astype(kind)


def heavy_noise(own_key, dims, width, bound, cuts, heavy, held_as=jnp.bfloat16):
    values = width * jax.random.normal(own_key, dims, jnp.float32)
    if cuts:
        values = values * shard_levels(own_key, dims, cuts, -0.22, 0.18)
    return jnp.clip(with_spikes(values, jax.random.fold_in(own_key, 3), *heavy), -bound, bound).astype(held_as)


def setup_inputs(seed: int = 0) -> dict:
    arg_keys = jax.random.split(jax.random.key(seed), 29)
    tokens = centred(arg_keys[0], (TOKENS, D), 1.0, 6.0, ((0, 32),))
    sequence_ids = draw_sequence_ids(jax.random.fold_in(arg_keys[28], 71), 0)
    sequence_offsets = draw_sequence_offsets(jax.random.fold_in(arg_keys[28], 71), 0)
    signed_norm_gain = jnp.clip(1.0 + 0.18 * jax.random.normal(arg_keys[3], (D,), jnp.float32), 0.099609375, 1.8984375).astype(jnp.bfloat16)
    signed_norm_bias = centred(arg_keys[4], (D,), 0.3, 1.75)
    signed_query = centred(arg_keys[5], (D, D), D ** -0.5, 0.21875)
    signed_key = centred(arg_keys[6], (D, D), D ** -0.5, 0.21875)
    signed_value = centred(arg_keys[7], (D, D), D ** -0.5, 0.21875)
    signed_out = centred(arg_keys[8], (D, D), (D // 64) ** -0.5, 1.75)
    signed_mlp_gain = jnp.clip(1.0 + 0.18 * jax.random.normal(arg_keys[9], (D,), jnp.float32), 0.099609375, 1.8984375).astype(jnp.bfloat16)
    signed_mlp_bias = centred(arg_keys[10], (D,), 0.3, 1.75)
    signed_up = centred(arg_keys[11], (D, FF), D ** -0.5, 0.21875)
    signed_up_bias = centred(arg_keys[12], (FF,), 0.5, 3.0)
    signed_down = centred(arg_keys[13], (FF, D), FF ** -0.5, 0.109375)
    signed_down_bias = centred(arg_keys[14], (D,), 0.3, 1.75)
    plain_norm_gain = jnp.clip(1.0 + 0.18 * jax.random.normal(arg_keys[15], (D,), jnp.float32), 0.099609375, 1.8984375).astype(jnp.bfloat16)
    plain_norm_bias = centred(arg_keys[16], (D,), 0.3, 1.75)
    plain_query = centred(arg_keys[17], (D, D), D ** -0.5, 0.21875)
    plain_key = centred(arg_keys[18], (D, D), D ** -0.5, 0.21875)
    plain_value = centred(arg_keys[19], (D, D), D ** -0.5, 0.21875)
    plain_out = centred(arg_keys[20], (D, D), (D // 64) ** -0.5, 1.75)
    plain_mlp_gain = jnp.clip(1.0 + 0.18 * jax.random.normal(arg_keys[21], (D,), jnp.float32), 0.099609375, 1.8984375).astype(jnp.bfloat16)
    plain_mlp_bias = centred(arg_keys[22], (D,), 0.3, 1.75)
    plain_up = centred(arg_keys[23], (D, FF), D ** -0.5, 0.21875)
    plain_up_bias = centred(arg_keys[24], (FF,), 0.5, 3.0)
    plain_down = centred(arg_keys[25], (FF, D), FF ** -0.5, 0.109375)
    plain_down_bias = centred(arg_keys[26], (D,), 0.3, 1.75)
    cotangent = heavy_noise(arg_keys[27], (TOKENS, D), 1.0, 6.0, ((0, 32),), (0, 1, 32, 2.75))
    return {"tokens": tokens, "sequence_ids": sequence_ids, "sequence_offsets": sequence_offsets, "signed_norm_gain": signed_norm_gain, "signed_norm_bias": signed_norm_bias, "signed_query": signed_query, "signed_key": signed_key, "signed_value": signed_value, "signed_out": signed_out, "signed_mlp_gain": signed_mlp_gain, "signed_mlp_bias": signed_mlp_bias, "signed_up": signed_up, "signed_up_bias": signed_up_bias, "signed_down": signed_down, "signed_down_bias": signed_down_bias, "plain_norm_gain": plain_norm_gain, "plain_norm_bias": plain_norm_bias, "plain_query": plain_query, "plain_key": plain_key, "plain_value": plain_value, "plain_out": plain_out, "plain_mlp_gain": plain_mlp_gain, "plain_mlp_bias": plain_mlp_bias, "plain_up": plain_up, "plain_up_bias": plain_up_bias, "plain_down": plain_down, "plain_down_bias": plain_down_bias, "cotangent": cotangent}


EPSILON = 1e-05
MASKED_FLOOR = -1e+30
PRECISE = lax.Precision.HIGHEST

@jax.custom_vjp
def low(v):
    return lax.optimization_barrier(v.astype(jnp.bfloat16)).astype(jnp.float32)

@jax.custom_vjp
def low_back(v):
    return v

def low_keep(v):
    return (low(v), None)

def low_pass(kept, grad):
    return (grad,)

def back_keep(v):
    return (v, None)

def back_low(kept, grad):
    return (low(grad),)
low.defvjp(low_keep, low_pass)
low_back.defvjp(back_keep, back_low)

def layer_norm(values, gain, shift):
    centre = values - lax.optimization_barrier(jnp.mean(values, axis=-1, keepdims=True))
    spread = lax.optimization_barrier(jnp.mean(centre * centre, axis=-1, keepdims=True))
    return centre * lax.rsqrt(spread + EPSILON) * gain + shift

def to_groups(stacked):
    group_rows = LONG // N_KA
    trailing = stacked.shape[1:]
    stacked = stacked.reshape((N_PB, N_KA, BATCH, group_rows) + trailing)
    stacked = jnp.moveaxis(stacked, 2, 1)
    return stacked.reshape((N_PB * BATCH, LONG) + trailing)

def from_groups(stacked):
    group_rows = LONG // N_KA
    trailing = stacked.shape[2:]
    stacked = stacked.reshape((N_PB, BATCH, N_KA, group_rows) + trailing)
    stacked = jnp.moveaxis(stacked, 1, 2)
    return stacked.reshape((N_PB * N_KA * BATCH * group_rows,) + trailing)

def group_attend(queries, key_vectors, values, labels, offsets, signed):
    score_scale = HEAD_DIM ** (-0.5)
    head_shape = (LONG, HEADS, HEAD_DIM)
    scores = jnp.einsum('qhd,khd->hqk', queries.reshape(head_shape), key_vectors.reshape(head_shape), precision=PRECISE) * score_scale
    scores = low_back(scores)
    allowed = (labels[:, None] == labels[None, :]) & (offsets[None, :] <= offsets[:, None])
    if signed:
        magnitude = jnp.sqrt(scores * scores + 1.0)
    else:
        magnitude = scores
    clipped = jnp.where(allowed, magnitude, MASKED_FLOOR)
    highest = lax.optimization_barrier(jnp.max(clipped, axis=-1, keepdims=True))
    raised = jnp.where(allowed, jnp.exp(clipped - highest), 0.0)
    weights = raised / lax.optimization_barrier(jnp.sum(raised, axis=-1, keepdims=True))
    if signed:
        weights = weights * scores / magnitude
    attended = jnp.einsum('hqk,khd->qhd', low(weights), values.reshape(head_shape), precision=PRECISE)
    return attended.reshape(LONG, HEADS * HEAD_DIM)

def attend(queries, key_vectors, values, labels, offsets, signed):
    group_step = jax.checkpoint(lambda packed: group_attend(packed[0], packed[1], packed[2], packed[3], packed[4], signed))
    grouped = (to_groups(queries), to_groups(key_vectors), to_groups(values), to_groups(labels), to_groups(offsets))
    return from_groups(lax.map(group_step, grouped))

def residual_block(current, params, labels, offsets, signed):
    norm_gain, norm_bias, w_query, w_key, w_value, w_out, mlp_gain, mlp_bias, w_up, up_bias, w_down, down_bias = params
    normed = low(layer_norm(current, norm_gain, norm_bias))
    queries = low(low_back(jnp.dot(normed, w_query, precision=PRECISE)))
    key_vectors = low(low_back(jnp.dot(normed, w_key, precision=PRECISE)))
    values = low(low_back(jnp.dot(normed, w_value, precision=PRECISE)))
    attended = low(low_back(attend(queries, key_vectors, values, labels, offsets, signed)))
    middle = current + low_back(jnp.dot(attended, w_out, precision=PRECISE))
    normed_mlp = low(layer_norm(middle, mlp_gain, mlp_bias))
    hidden = low_back(jnp.dot(normed_mlp, w_up, precision=PRECISE) + up_bias)
    active = low(jax.nn.gelu(hidden, approximate=False))
    return middle + low_back(jnp.dot(active, w_down, precision=PRECISE) + down_bias)

def reference(tokens, sequence_ids, sequence_offsets, signed_norm_gain, signed_norm_bias, signed_query, signed_key, signed_value, signed_out, signed_mlp_gain, signed_mlp_bias, signed_up, signed_up_bias, signed_down, signed_down_bias, plain_norm_gain, plain_norm_bias, plain_query, plain_key, plain_value, plain_out, plain_mlp_gain, plain_mlp_bias, plain_up, plain_up_bias, plain_down, plain_down_bias, cotangent):
    signed_params = [weight.astype(jnp.float32) for weight in (signed_norm_gain, signed_norm_bias, signed_query, signed_key, signed_value, signed_out, signed_mlp_gain, signed_mlp_bias, signed_up, signed_up_bias, signed_down, signed_down_bias)]
    plain_params = [weight.astype(jnp.float32) for weight in (plain_norm_gain, plain_norm_bias, plain_query, plain_key, plain_value, plain_out, plain_mlp_gain, plain_mlp_bias, plain_up, plain_up_bias, plain_down, plain_down_bias)]

    def forward(current, first_layer, second_layer):
        current = residual_block(current, first_layer, sequence_ids, sequence_offsets, True)
        return residual_block(current, second_layer, sequence_ids, sequence_offsets, False)
    result, pullback = jax.vjp(forward, tokens.astype(jnp.float32), signed_params, plain_params)
    back_input, back_signed, back_plain = pullback(cotangent.astype(jnp.float32))
    return (result.astype(jnp.bfloat16), back_input, back_signed[0], back_signed[1], back_signed[2], back_signed[3], back_signed[4], back_signed[5], back_signed[6], back_signed[7], back_signed[8], back_signed[9], back_signed[10], back_signed[11], back_plain[0], back_plain[1], back_plain[2], back_plain[3], back_plain[4], back_plain[5], back_plain[6], back_plain[7], back_plain[8], back_plain[9], back_plain[10], back_plain[11])
```

```python
import functools

import jax
import jax.numpy as jnp
from jax import lax
from jax.experimental import pallas as pl
from jax.experimental.pallas import tpu as pltpu
from jax.sharding import PartitionSpec as P

HEADS = 12
BATCH = 2
HALVES = 2
OWN = BATCH * HALVES
EPSILON = 1e-05
FLOOR = -1e30
BF = jnp.bfloat16
F32 = jnp.float32
MIB = 1 << 20

NT = (((1,), (1,)), ((), ()))
NN = (((1,), (0,)), ((), ()))
TN = (((0,), (0,)), ((), ()))


def dot(left, right, dims=NN):
    return lax.dot_general(left, right, dims, preferred_element_type=F32)


def dense(left, right, left_axis, right_axis):
    return lax.dot_general(
        left, right, (((left_axis,), (right_axis,)), ((), ())), preferred_element_type=F32
    )


def attention_sizes(width):
    head = width // HEADS
    lanes = 256
    while width % lanes or lanes % head:
        lanes //= 2
    return head, lanes, width // lanes, lanes // head


def head_parts(block, head, count):
    lane = lax.broadcasted_iota(jnp.int32, block.shape, 1) // head
    return [jnp.where(lane == h, block, jnp.zeros_like(block)) for h in range(count)]


def turned(block):
    return jnp.transpose(block.astype(F32))


def causal(shape):
    key = lax.broadcasted_iota(jnp.int32, shape, 0)
    query = lax.broadcasted_iota(jnp.int32, shape, 1)
    return key <= query


def forward_kernel(head, count, signed, bounds, q_ref, k_ref, v_ref, o_ref, lse_ref, qm, vt, acc):
    step = pl.program_id(1)

    @pl.when(step == 0)
    def _():
        for j in range(k_ref.shape[0]):
            vt[j] = turned(v_ref[j]).astype(BF)

    for h, part in enumerate(head_parts(q_ref[0], head, count)):
        qm[h] = part
    acc[...] = jnp.zeros_like(acc)
    rows = q_ref.shape[1]
    start, last = bounds[0, step], bounds[1, step]

    def block(j, carry, masked):
        keys = k_ref[j]
        result = []
        for h in range(count):
            top, total = carry[2 * h], carry[2 * h + 1]
            s = dot(keys, qm[h], NT)
            if signed:
                square = s * s + 1.0
                inverse = lax.rsqrt(square)
                c = square * inverse
            else:
                c = s
            if masked:
                c = jnp.where(causal(c.shape), c, FLOOR)
            higher = jnp.maximum(top, jnp.max(c, axis=0, keepdims=True))
            raised = jnp.exp(c - higher)
            fade = jnp.exp(top - higher)
            total = total * fade + jnp.sum(raised, axis=0, keepdims=True)
            if signed:
                raised = raised * (s * inverse)
            part = dot(vt[j, h * head : (h + 1) * head, :], raised.astype(BF))
            acc[h] = acc[h] * fade + part
            result += [higher, total]
        return tuple(result)

    first = (jnp.full((1, rows), FLOOR, F32), jnp.zeros((1, rows), F32)) * count
    carry = lax.fori_loop(start, last, lambda j, c: block(j, c, False), first)
    carry = block(last, carry, True)
    for h in range(count):
        top, total = carry[2 * h], carry[2 * h + 1]
        acc[h] = acc[h] / total
        lse_ref[0, h : h + 1, :] = top + jnp.log(total)
    o_ref[0] = jnp.transpose(acc[...].reshape(count * head, rows)).astype(BF)


def attend_forward(queries, keys, values, bounds, signed):
    pieces, rows, width = queries.shape
    whole = keys.shape[0]
    head, lanes, groups, count = attention_sizes(width)
    return pl.pallas_call(
        functools.partial(forward_kernel, head, count, signed),
        out_shape=(
            jax.ShapeDtypeStruct(queries.shape, BF),
            jax.ShapeDtypeStruct((pieces * groups, count, rows), F32),
        ),
        grid_spec=pltpu.PrefetchScalarGridSpec(
            num_scalar_prefetch=1,
            grid=(groups, pieces),
            in_specs=[
                pl.BlockSpec((1, rows, lanes), lambda g, i, b: (i, 0, g)),
                pl.BlockSpec((whole, rows, lanes), lambda g, i, b: (0, 0, g)),
                pl.BlockSpec((whole, rows, lanes), lambda g, i, b: (0, 0, g)),
            ],
            out_specs=[
                pl.BlockSpec((1, rows, lanes), lambda g, i, b: (i, 0, g)),
                pl.BlockSpec((1, count, rows), lambda g, i, b: (g * pieces + i, 0, 0)),
            ],
            scratch_shapes=[
                pltpu.VMEM((count, rows, lanes), BF),
                pltpu.VMEM((whole, lanes, rows), BF),
                pltpu.VMEM((count, head, rows), F32),
            ],
        ),
        compiler_params=pltpu.CompilerParams(vmem_limit_bytes=48 * MIB),
    )(bounds, queries, keys, values)


def backward_kernel(
    head, count, signed, bounds, q_ref, do_ref, o_ref, lse_ref, k_ref, v_ref,
    dq_ref, dk_ref, dv_ref, qm, dom, kt, dq, dk, dv, delta,
):
    step = pl.program_id(1)
    whole, rows, lanes = k_ref.shape

    @pl.when(step == 0)
    def _():
        for j in range(whole):
            kt[j] = turned(k_ref[j]).astype(BF)
            dk[j] = jnp.zeros((rows, lanes), F32)
            dv[j] = jnp.zeros((rows, lanes), F32)

    for h, part in enumerate(head_parts(q_ref[0], head, count)):
        qm[h] = part
    for h, part in enumerate(head_parts(do_ref[0], head, count)):
        dom[h] = part
    product = jnp.transpose(do_ref[0].astype(F32) * o_ref[0].astype(F32))
    for h in range(count):
        delta[h : h + 1, :] = jnp.sum(product[h * head : (h + 1) * head], axis=0, keepdims=True)
    dq[...] = jnp.zeros_like(dq)
    start, last = bounds[0, step], bounds[1, step]

    def block(j, masked):
        keys, values = k_ref[j], v_ref[j]
        dk_part = dv_part = None
        for h in range(count):
            s = dot(keys, qm[h], NT)
            dp = dot(values, dom[h], NT)
            if signed:
                square = s * s + 1.0
                inverse = lax.rsqrt(square)
                c = square * inverse
            else:
                c = s
            if masked:
                c = jnp.where(causal(c.shape), c, FLOOR)
            w = jnp.exp(c - lse_ref[0, h : h + 1, :])
            if signed:
                ratio = s * inverse
                p = w * ratio
                squared = inverse * inverse
                slope = 1.0 + squared * (inverse - 1.0)
                ds = w * (dp * slope - delta[h : h + 1, :] * ratio)
            else:
                p = w
                ds = w * (dp - delta[h : h + 1, :])
            p, ds = p.astype(BF), ds.astype(BF)
            dq[h] += dot(kt[j, h * head : (h + 1) * head, :], ds)
            dv_h, dk_h = dot(p, dom[h]), dot(ds, qm[h])
            dk_part = dk_h if dk_part is None else dk_part + dk_h
            dv_part = dv_h if dv_part is None else dv_part + dv_h
        dk[j] += dk_part
        dv[j] += dv_part

    @pl.loop(start, last)
    def _(j):
        block(j, False)

    block(last, True)
    turned_back = jnp.transpose(dq[...].reshape(count * head, rows)) * (head ** -0.5)
    dq_ref[0] = turned_back.astype(BF)

    @pl.when(step == pl.num_programs(1) - 1)
    def _():
        for j in range(whole):
            dk_ref[j] = dk[j].astype(BF)
            dv_ref[j] = dv[j].astype(BF)


def attend_backward(queries, grad_rows, attended, totals, keys, values, bounds, signed):
    pieces, rows, width = queries.shape
    whole = keys.shape[0]
    head, lanes, groups, count = attention_sizes(width)
    own = pl.BlockSpec((1, rows, lanes), lambda g, i, b: (i, 0, g))
    every = pl.BlockSpec((whole, rows, lanes), lambda g, i, b: (0, 0, g))
    return pl.pallas_call(
        functools.partial(backward_kernel, head, count, signed),
        out_shape=(
            jax.ShapeDtypeStruct(queries.shape, BF),
            jax.ShapeDtypeStruct(keys.shape, BF),
            jax.ShapeDtypeStruct(keys.shape, BF),
        ),
        grid_spec=pltpu.PrefetchScalarGridSpec(
            num_scalar_prefetch=1,
            grid=(groups, pieces),
            in_specs=[
                own,
                own,
                own,
                pl.BlockSpec((1, count, rows), lambda g, i, b: (g * pieces + i, 0, 0)),
                every,
                every,
            ],
            out_specs=[own, every, every],
            scratch_shapes=[
                pltpu.VMEM((count, rows, lanes), BF),
                pltpu.VMEM((count, rows, lanes), BF),
                pltpu.VMEM((whole, lanes, rows), BF),
                pltpu.VMEM((count, head, rows), F32),
                pltpu.VMEM((whole, rows, lanes), F32),
                pltpu.VMEM((whole, rows, lanes), F32),
                pltpu.VMEM((count, rows), F32),
            ],
        ),
        compiler_params=pltpu.CompilerParams(vmem_limit_bytes=56 * MIB),
    )(bounds, queries, grad_rows, attended, totals, keys, values)


def xor_send(array, axis, bit):
    size = lax.axis_size(axis)
    return lax.ppermute(array, axis, [(i, i ^ bit) for i in range(size)])


def shift_send(array, shift):
    size = lax.axis_size("ka")
    return lax.ppermute(array, "ka", [(i, (i + shift) % size) for i in range(size)])


def pick(array, index, axis=0):
    return lax.dynamic_index_in_dim(array, index, axis, keepdims=False)


def member_send(array, offset):
    if offset & 1:
        array = xor_send(array, "pb", 1)
    if offset >> 1:
        array = xor_send(array, "ka", offset >> 1)
    return array


def share_with_group(array, members):
    return jnp.concatenate([array] + [member_send(array, e) for e in range(1, members)], axis=0)


class Layout:
    def __init__(self, sequence_ids, sequence_offsets):
        self.core = lax.axis_index("pb") % 2
        self.z = lax.axis_index("ka")
        self.depth = lax.axis_size("ka")
        self.subs = self.depth // 4
        self.members = self.depth // 2
        tall = sequence_ids.shape[0]
        self.rows = tall // OWN
        long = tall // BATCH * self.depth
        heads = slice(None, None, self.rows)
        keys = sequence_ids[heads] * long + sequence_offsets[heads]
        keys = jnp.broadcast_to(keys.reshape(BATCH, HALVES, 1), (BATCH, HALVES, self.subs))
        keys = self.gather_in(keys)[:, 0]
        count = keys.shape[0]
        rank = jnp.sum(keys[None, :] < keys[:, None], axis=1)
        places = jnp.arange(count)
        self.by_rank = jnp.sum(
            jnp.where(rank[None, :] == places[:, None], places[None, :], 0), axis=1
        )
        self.short = jnp.max(keys) // long != jnp.min(keys) // long
        self.member = (self.z % self.subs) * 2 + self.core
        ranks = self.ranks_of(self.member)
        self.ranks = ranks
        start = jnp.where(self.short, ranks // (count // 2) * (count // 2), 0)
        self.bounds = jnp.stack([start, ranks]).astype(jnp.int32)
        held = jnp.concatenate([self.ranks_of(self.member ^ e) for e in range(self.members)])
        self.held_ranks = held
        self.held_by_rank = jnp.sum(
            jnp.where(held[None, :] == places[:, None], places[None, :], 0), axis=1
        )

    def ranks_of(self, member):
        n = self.members
        m = n // 2

        def spread(e, size):
            return jnp.stack([e, 2 * size - 1 - e, 2 * size + e, 4 * size - 1 - e])

        return jnp.where(
            self.short, member // m * (2 * n) + spread(member % m, m), spread(member, n)
        )

    def gather_in(self, array):
        kept, sent = pick(array, self.core, 1), pick(array, 1 - self.core, 1)
        four = jnp.concatenate([kept, xor_send(sent, "pb", 1)], axis=0)
        four = four.reshape((4, self.subs, four.shape[1] // self.subs) + four.shape[2:])
        parts = []
        for shift in range(self.depth):
            target = (self.z + shift) % self.depth
            group, sub = target // self.subs, target % self.subs
            slot = (group // 2 ^ self.core) * 2 + group % 2
            part = pick(pick(four, slot), sub)
            parts.append(shift_send(part, shift) if shift else part)
        held = jnp.stack(parts)
        if self.subs > 1:
            held = jnp.take(held, (self.z - jnp.arange(self.depth)) % self.depth, axis=0)
        held = jnp.stack([held, xor_send(held, "pb", 1)])
        if self.subs > 1:
            groups = [
                [g * self.subs + i for i in range(self.subs)] for g in range(4)
            ]
            held = lax.all_gather(held, "ka", axis=2, axis_index_groups=groups)
            held = held.reshape(held.shape[:2] + (held.shape[2] * held.shape[3],) + held.shape[4:])
        return held.reshape((2 * self.depth,) + held.shape[2:])

    def scatter_out(self, own):
        shared = share_with_group(own, self.members)
        rows, width = own.shape[1:]
        piece = rows // self.subs
        got = []
        for shift in range(self.depth):
            index = shift if self.subs == 1 else (self.z - shift) % self.depth
            place = pick(self.held_by_rank, pick(self.rank_of_piece, index))
            part = pick(shared, place)
            if self.subs > 1:
                part = pick(part.reshape(self.subs, piece, width), self.z % self.subs)
            got.append(shift_send(part, -shift) if shift else part)
        table = jnp.stack(got)
        order = []
        for slot in range(4):
            group = ((slot // 2) ^ self.core) * 2 + slot % 2
            for sub in range(self.subs):
                order.append((group * self.subs + sub - self.z) % self.depth)
        four = jnp.take(table, jnp.stack(order), axis=0).reshape(4, rows, width)
        mine, given = four[:2], xor_send(four[2:], "pb", 1)
        first = self.core == 0
        low = jnp.where(first, mine, given)
        high = jnp.where(first, given, mine)
        return jnp.stack([low, high], axis=1).reshape(BATCH * HALVES * rows, width)

    @property
    def rank_of_piece(self):
        places = jnp.arange(self.by_rank.shape[0])
        return jnp.sum(
            jnp.where(self.by_rank[None, :] == places[:, None], places[None, :], 0), axis=1
        )


def reduce_matrix(gradient, order):
    height, breadth = gradient.shape
    along_pb, along_ka = lax.axis_size("pb"), lax.axis_size("ka")
    bits = along_pb.bit_length() - 1
    place = lax.axis_index("pb")
    view = gradient.astype(BF).reshape((2,) * bits + (height // along_pb, breadth))
    steps = [0] + [b for b in range(1, bits)][::order]
    for b in steps:
        axis = bits - 1 - b
        own = (place >> b) & 1
        kept = lax.dynamic_slice_in_dim(view, own, 1, axis)
        sent = lax.dynamic_slice_in_dim(view, 1 - own, 1, axis)
        view = kept + xor_send(sent, "pb", 1 << b)
    block = view.reshape(height // along_pb, breadth)
    wide = breadth // along_ka
    z = lax.axis_index("ka")
    total = lax.dynamic_slice_in_dim(block, z * wide, wide, 1).astype(F32)
    for shift in range(1, along_ka):
        part = lax.dynamic_slice_in_dim(block, (z + shift) % along_ka * wide, wide, 1)
        total = total + shift_send(part, shift).astype(F32)
    return total


def reduce_vectors(vectors):
    sizes = [v.shape[0] for v in vectors]
    flat = jnp.concatenate(vectors).reshape(-1, 128)
    for axis in ("pb", "ka"):
        bit = 1
        while bit < lax.axis_size(axis):
            flat = flat + xor_send(flat, axis, bit)
            bit *= 2
    flat = flat.reshape(-1)
    result, at = [], 0
    for size in sizes:
        result.append(flat[at : at + size])
        at += size
    return result


def normalized(values):
    centre = values - jnp.mean(values, axis=-1, keepdims=True)
    spread = jnp.mean(centre * centre, axis=-1, keepdims=True)
    scale = lax.rsqrt(spread + EPSILON)
    return centre * scale, scale


def layer_norm(values, gain, shift):
    return (normalized(values)[0] * gain.astype(F32) + shift.astype(F32)).astype(BF)


def norm_backward(values, gain, upstream):
    n, scale = normalized(values)
    grad_gain = jnp.sum(upstream * n, axis=0)
    grad_shift = jnp.sum(upstream, axis=0)
    dn = upstream * gain.astype(F32)
    mean = jnp.mean(dn, axis=-1, keepdims=True)
    along = jnp.mean(dn * n, axis=-1, keepdims=True)
    return scale * (dn - mean - n * along), grad_gain, grad_shift


def gelu_pair(u):
    size = jnp.abs(u) * 0.7071067811865476
    t = 1.0 / (1.0 + 0.3275911 * size)
    bell = jnp.exp(-0.5 * u * u)
    series = t * (
        0.254829592
        + t * (-0.284496736 + t * (1.421413741 + t * (-1.453152027 + t * 1.061405429)))
    )
    tail = 0.5 * series * bell
    phi = jnp.where(u < 0, tail, 1.0 - tail)
    return u * phi, phi + u * (bell * 0.3989422804014327)


def layer_forward(x_own, h_own, h_all, params, layout, signed):
    (_, _, w_query, w_key, w_value, w_out, mlp_gain, mlp_bias, w_up, up_bias, w_down, down_bias) = params
    width = x_own.shape[1]
    rows = layout.rows
    scale = (width // HEADS) ** -0.5
    queries = (dense(h_own, w_query, 1, 0) * scale).astype(BF).reshape(OWN, rows, width)
    keys = dense(h_all, w_key, 1, 0).astype(BF).reshape(-1, rows, width)
    values = dense(h_all, w_value, 1, 0).astype(BF).reshape(-1, rows, width)
    attended, totals = attend_forward(queries, keys, values, layout.bounds, signed)
    middle = x_own + dense(attended.reshape(-1, width), w_out, 1, 0)
    h2 = layer_norm(middle, mlp_gain, mlp_bias)
    hidden = dense(h2, w_up, 1, 0) + up_bias.astype(F32)
    active, slope = gelu_pair(hidden)
    active, slope = active.astype(BF), slope.astype(BF)
    result = middle + (dense(active, w_down, 1, 0) + down_bias.astype(F32))
    return result, (h_own, h_all, queries, keys, values, attended, totals, middle, h2, active, slope)


def layer_backward(upstream, x_own, params, saved, layout, signed):
    (norm_gain, _, w_query, w_key, w_value, w_out, mlp_gain, _, w_up, _, w_down, _) = params
    h_own, h_all, queries, keys, values, attended, totals, middle, h2, active, slope = saved
    tall, width = x_own.shape
    rows = layout.rows
    gb = upstream.astype(BF)
    grad_down_bias = jnp.sum(gb.astype(F32), axis=0)
    grad_down = dense(active, gb, 0, 0)
    du = (dense(gb, w_down, 1, 1) * slope.astype(F32)).astype(BF)
    grad_up_bias = jnp.sum(du.astype(F32), axis=0)
    grad_up = dense(h2, du, 0, 0)
    dh2 = dense(du, w_up, 1, 1)
    dx1, grad_mlp_gain, grad_mlp_bias = norm_backward(middle, mlp_gain, dh2)
    dx1 = upstream + dx1
    gx = dx1.astype(BF)
    grad_out = dense(attended.reshape(tall, width), gx, 0, 0)
    do = dense(gx, w_out, 1, 1).astype(BF).reshape(queries.shape)
    dq, dk, dv = attend_backward(
        queries, do, attended, totals, keys, values, layout.bounds, signed
    )
    dq, dk, dv = dq.reshape(tall, width), dk.reshape(-1, width), dv.reshape(-1, width)
    grad_query = dense(h_own, dq, 0, 0)
    grad_key = dense(h_all, dk, 0, 0)
    grad_value = dense(h_all, dv, 0, 0)
    from_keys = dense(dk, w_key, 1, 1) + dense(dv, w_value, 1, 1)
    from_keys = from_keys.astype(BF).reshape(-1, rows, width)
    by_member = jnp.take(from_keys, layout.held_ranks, axis=0).reshape(
        layout.members, tall, width
    )
    dh = dense(dq, w_query, 1, 1) + by_member[0].astype(F32)
    for e in range(1, layout.members):
        dh = dh + member_send(by_member[e], e).astype(F32)
    dx, grad_norm_gain, grad_norm_bias = norm_backward(x_own, norm_gain, dh)
    matrices = (grad_query, grad_key, grad_value, grad_out, grad_up, grad_down)
    orders = (1, -1, 1, -1, 1, -1)
    matrices = [reduce_matrix(g, o) for g, o in zip(matrices, orders)]
    vectors = (grad_norm_gain, grad_norm_bias, grad_mlp_gain, grad_mlp_bias, grad_up_bias, grad_down_bias)
    vectors = reduce_vectors(vectors)
    gradients = (
        vectors[0], vectors[1], matrices[0], matrices[1], matrices[2], matrices[3],
        vectors[2], vectors[3], matrices[4], vectors[4], matrices[5], vectors[5],
    )
    return dx1 + dx, gradients


def per_device(tokens, sequence_ids, sequence_offsets, *rest):
    signed_params, plain_params, cotangent = rest[:12], rest[12:24], rest[24]
    tall, width = tokens.shape
    layout = Layout(sequence_ids, sequence_offsets)
    shape = (BATCH, HALVES, layout.rows, width)
    x_all = layout.gather_in(tokens.reshape(shape))
    x_sorted = jnp.take(x_all, layout.by_rank, axis=0)
    h_sorted = layer_norm(x_sorted.astype(F32), signed_params[0], signed_params[1])
    x_own = jnp.take(x_sorted, layout.ranks, axis=0).reshape(tall, width).astype(F32)
    h_own = jnp.take(h_sorted, layout.ranks, axis=0).reshape(tall, width)
    between, signed_saved = layer_forward(
        x_own, h_own, h_sorted.reshape(-1, width), signed_params, layout, True
    )
    h_own = layer_norm(between, plain_params[0], plain_params[1])
    h_all = share_with_group(h_own.reshape(OWN, layout.rows, width), layout.members)
    h_all = jnp.take(h_all, layout.held_by_rank, axis=0).reshape(-1, width)
    final, plain_saved = layer_forward(between, h_own, h_all, plain_params, layout, False)
    output = layout.scatter_out(final.astype(BF).reshape(OWN, layout.rows, width))
    own_pieces = jnp.take(layout.by_rank, layout.ranks)
    upstream = jnp.take(layout.gather_in(cotangent.reshape(shape)), own_pieces, axis=0)
    upstream = upstream.reshape(tall, width).astype(F32)
    upstream, plain_grads = layer_backward(
        upstream, between, plain_params, plain_saved, layout, False
    )
    upstream, signed_grads = layer_backward(
        upstream, x_own, signed_params, signed_saved, layout, True
    )
    back = layout.scatter_out(upstream.astype(BF).reshape(OWN, layout.rows, width))
    return (output, back.astype(F32)) + signed_grads + plain_grads


def solution(mesh):
    rows, block = P(("pb", "ka"), None), P("pb", "ka")
    grads = (P(), P(), block, block, block, block, P(), P(), block, P(), block, P())
    return jax.shard_map(
        per_device,
        mesh=mesh,
        in_specs=(rows, P(("pb", "ka")), P(("pb", "ka"))) + (P(),) * 24 + (rows,),
        out_specs=(rows, rows) + grads + grads,
        check_vma=False,
    )
```

```python
import functools

import jax
import jax.numpy as jnp
from jax import lax
from jax.experimental import pallas as pl
from jax.experimental.pallas import tpu as pltpu
from jax.sharding import PartitionSpec as P

HEADS = 12
BATCH = 2
HALVES = 2
OWN = BATCH * HALVES
EPSILON = 1e-05
FLOOR = -1e30
LEAST, MOST = 1e-25, 1e30
BF = jnp.bfloat16
F32 = jnp.float32
MIB = 1 << 20

NT = (((1,), (1,)), ((), ()))
NN = (((1,), (0,)), ((), ()))
TN = (((0,), (0,)), ((), ()))


def dot(left, right, dims=NN):
    return lax.dot_general(left, right, dims, preferred_element_type=F32)


def dense(left, right, left_axis, right_axis):
    return lax.dot_general(
        left, right, (((left_axis,), (right_axis,)), ((), ())), preferred_element_type=F32
    )


def attention_sizes(width):
    head = width // HEADS
    lanes = 256
    while width % lanes or lanes % head:
        lanes //= 2
    return head, lanes, width // lanes, lanes // head


def head_parts(block, head, count):
    tile = min(128, block.shape[1])
    per = tile // head
    lane = lax.broadcasted_iota(jnp.int32, (block.shape[0], tile), 1) // head
    tiles = [block[:, t : t + tile] for t in range(0, block.shape[1], tile)]
    zero = jnp.zeros_like(tiles[0])
    return [jnp.where(lane == h % per, tiles[h // per], zero) for h in range(count)]


def tiles_of(block, head, count):
    tile = min(128, block.shape[1])
    per = tile // head
    tiles = [block[:, t : t + tile] for t in range(0, block.shape[1], tile)]
    return [tiles[h // per] for h in range(count)]


def join_tiles(parts, head):
    per = parts[0].shape[1] // head
    sums = [sum(parts[h + 1 : h + per], parts[h]) for h in range(0, len(parts), per)]
    return sums[0] if len(sums) == 1 else jnp.concatenate(sums, axis=1)


def turned(block):
    return jnp.transpose(block.astype(F32))


def causal(shape):
    key = lax.broadcasted_iota(jnp.int32, shape, 0)
    query = lax.broadcasted_iota(jnp.int32, shape, 1)
    return key <= query


def forward_kernel(head, count, signed, bounds, order, q_ref, k_ref, v_ref, o_ref, lse_ref, qm, vt, acc, sums):
    step = pl.program_id(1)

    @pl.when(step == 0)
    def _():
        for j in range(k_ref.shape[0]):
            vt[j] = turned(v_ref[j]).astype(BF)

    for h, part in enumerate(head_parts(q_ref[0], head, count)):
        qm[h] = part
    rows = q_ref.shape[1]
    start, last = bounds[step], bounds[OWN + step]

    def scores(j):
        return [dot(keys, qm[h], NT) for h, keys in enumerate(tiles_of(k_ref[j], head, count))]

    def magnitude(s, masked):
        c, ratio = s, None
        if signed:
            square = s * s + 1.0
            inverse = lax.rsqrt(square)
            c, ratio = square * inverse, s * inverse
        if masked:
            c = jnp.where(causal(c.shape), c, FLOOR)
        return c, ratio

    def weigh(j, h, raised, ratio):
        if signed:
            raised = raised * ratio
        return dot(vt[j, h * head : (h + 1) * head, :], raised.astype(BF))

    def plain_block(j, carry, masked):
        result = []
        for h, s in enumerate(scores(j)):
            c, ratio = magnitude(s, masked)
            raised = jnp.exp(c)
            result.append(carry[h] + jnp.sum(raised, axis=0, keepdims=True))
            acc[h] += weigh(j, h, raised, ratio)
        return tuple(result)

    def safe_block(j, carry, masked):
        result = []
        for h, s in enumerate(scores(j)):
            top, total = carry[2 * h], carry[2 * h + 1]
            c, ratio = magnitude(s, masked)
            higher = jnp.maximum(top, jnp.max(c, axis=0, keepdims=True))
            raised = jnp.exp(c - higher)
            fade = jnp.exp(top - higher)
            acc[h] = acc[h] * fade + weigh(j, h, raised, ratio)
            result += [higher, total * fade + jnp.sum(raised, axis=0, keepdims=True)]
        return tuple(result)

    def over_keys(block, first):
        acc[...] = jnp.zeros_like(acc)
        carry = lax.fori_loop(start, last, lambda j, c: block(order[j], c, False), first)
        return block(step, carry, True)

    zeros = jnp.zeros((1, rows), F32)
    totals = jnp.concatenate(over_keys(plain_block, (zeros,) * count), axis=0)
    fine = jnp.min(jnp.where((totals > LEAST) & (totals < MOST), 1.0, 0.0)) > 0.5
    sums[...] = totals
    lse_ref[0] = jnp.log(totals)

    @pl.when(jnp.logical_not(fine))
    def _():
        carry = over_keys(safe_block, (zeros + FLOOR, zeros) * count)
        for h in range(count):
            sums[h : h + 1, :] = carry[2 * h + 1]
            lse_ref[0, h : h + 1, :] = carry[2 * h] + jnp.log(carry[2 * h + 1])

    share = 1.0 / sums[...]
    for h in range(count):
        acc[h] = acc[h] * share[h : h + 1, :]
    o_ref[0] = jnp.transpose(acc[...].reshape(count * head, rows)).astype(BF)


def attend_forward(queries, keys, values, tables, signed):
    pieces, rows, width = queries.shape
    whole = keys.shape[0]
    head, lanes, groups, count = attention_sizes(width)
    return pl.pallas_call(
        functools.partial(forward_kernel, head, count, signed),
        out_shape=(
            jax.ShapeDtypeStruct(queries.shape, BF),
            jax.ShapeDtypeStruct((pieces * groups, count, rows), F32),
        ),
        grid_spec=pltpu.PrefetchScalarGridSpec(
            num_scalar_prefetch=2,
            grid=(groups, pieces),
            in_specs=[
                pl.BlockSpec((1, rows, lanes), lambda g, i, b, o: (i, 0, g)),
                pl.BlockSpec((whole, rows, lanes), lambda g, i, b, o: (0, 0, g)),
                pl.BlockSpec((whole, rows, lanes), lambda g, i, b, o: (0, 0, g)),
            ],
            out_specs=[
                pl.BlockSpec((1, rows, lanes), lambda g, i, b, o: (i, 0, g)),
                pl.BlockSpec((1, count, rows), lambda g, i, b, o: (g * pieces + i, 0, 0)),
            ],
            scratch_shapes=[
                pltpu.VMEM((count, rows, min(128, lanes)), BF),
                pltpu.VMEM((whole, lanes, rows), BF),
                pltpu.VMEM((count, head, rows), F32),
                pltpu.VMEM((count, rows), F32),
            ],
        ),
        compiler_params=pltpu.CompilerParams(vmem_limit_bytes=20 * MIB),
        cost_estimate=pl.CostEstimate(flops=50_000_000_000, bytes_accessed=20_000_000, transcendentals=0),
    )(*tables, queries, keys, values)


def backward_kernel(
    head, count, signed, bounds, order, q_ref, do_ref, o_ref, lse_ref, k_ref, v_ref,
    dq_ref, dk_ref, dv_ref, qm, dom, kt, dq, dk, dv, delta,
):
    step = pl.program_id(1)
    whole, rows, lanes = k_ref.shape

    @pl.when(step == 0)
    def _():
        for j in range(whole):
            kt[j] = turned(k_ref[j]).astype(BF)
            dk[j] = jnp.zeros((rows, lanes), F32)
            dv[j] = jnp.zeros((rows, lanes), F32)

    for h, part in enumerate(head_parts(q_ref[0], head, count)):
        qm[h] = part
    for h, part in enumerate(head_parts(do_ref[0], head, count)):
        dom[h] = part
    product = jnp.transpose(do_ref[0].astype(F32) * o_ref[0].astype(F32))
    for h in range(count):
        delta[h : h + 1, :] = jnp.sum(product[h * head : (h + 1) * head], axis=0, keepdims=True)
    dq[...] = jnp.zeros_like(dq)
    start, last = bounds[step], bounds[OWN + step]

    def block(j, masked):
        keys, values = tiles_of(k_ref[j], head, count), tiles_of(v_ref[j], head, count)
        heads = range(count)
        scores = [dot(keys[h], qm[h], NT) for h in heads]
        dps = [dot(values[h], dom[h], NT) for h in heads]
        ps, dss = [], []
        for h, s, dp in zip(heads, scores, dps):
            if signed:
                square = s * s + 1.0
                inverse = lax.rsqrt(square)
                c = square * inverse
            else:
                c = s
            if masked:
                c = jnp.where(causal(c.shape), c, FLOOR)
            w = jnp.exp(c - lse_ref[0, h : h + 1, :])
            if signed:
                ratio = s * inverse
                slope = 1.0 + inverse * inverse * (inverse - 1.0)
                ps.append((w * ratio).astype(BF))
                dss.append((w * (dp * slope - delta[h : h + 1, :] * ratio)).astype(BF))
            else:
                ps.append(w.astype(BF))
                dss.append((w * (dp - delta[h : h + 1, :])).astype(BF))
        dvs, dks = [], []
        for h, p, ds in zip(heads, ps, dss):
            dvs.append(dot(p, dom[h]))
            dks.append(dot(ds, qm[h]))
            dq[h] += dot(kt[j, h * head : (h + 1) * head, :], ds)
        dv[j] += join_tiles(dvs, head)
        dk[j] += join_tiles(dks, head)

    @pl.loop(start, last)
    def _(j):
        block(order[j], False)

    block(step, True)
    turned_back = jnp.transpose(dq[...].reshape(count * head, rows)) * (head ** -0.5)
    dq_ref[0] = turned_back.astype(BF)

    @pl.when(step == pl.num_programs(1) - 1)
    def _():
        for j in range(whole):
            dk_ref[j] = dk[j].astype(BF)
            dv_ref[j] = dv[j].astype(BF)


def attend_backward(queries, grad_rows, attended, totals, keys, values, tables, signed, first, end):
    pieces, rows, width = queries.shape
    whole = keys.shape[0]
    head, lanes, groups, count = attention_sizes(width)
    own = pl.BlockSpec((1, rows, lanes), lambda g, i, b, o: (i, 0, g + first))
    every = pl.BlockSpec((whole, rows, lanes), lambda g, i, b, o: (0, 0, g + first))
    own_out = pl.BlockSpec((1, rows, lanes), lambda g, i, b, o: (i, 0, g))
    every_out = pl.BlockSpec((whole, rows, lanes), lambda g, i, b, o: (0, 0, g))
    spread = (end - first) * lanes
    return pl.pallas_call(
        functools.partial(backward_kernel, head, count, signed),
        out_shape=(
            jax.ShapeDtypeStruct((pieces, rows, spread), BF),
            jax.ShapeDtypeStruct((whole, rows, spread), BF),
            jax.ShapeDtypeStruct((whole, rows, spread), BF),
        ),
        grid_spec=pltpu.PrefetchScalarGridSpec(
            num_scalar_prefetch=2,
            grid=(end - first, pieces),
            in_specs=[
                own,
                own,
                own,
                pl.BlockSpec((1, count, rows), lambda g, i, b, o: ((g + first) * pieces + i, 0, 0)),
                every,
                every,
            ],
            out_specs=[own_out, every_out, every_out],
            scratch_shapes=[
                pltpu.VMEM((count, rows, min(128, lanes)), BF),
                pltpu.VMEM((count, rows, min(128, lanes)), BF),
                pltpu.VMEM((whole, lanes, rows), BF),
                pltpu.VMEM((count, head, rows), F32),
                pltpu.VMEM((whole, rows, lanes), F32),
                pltpu.VMEM((whole, rows, lanes), F32),
                pltpu.VMEM((count, rows), F32),
            ],
        ),
        compiler_params=pltpu.CompilerParams(vmem_limit_bytes=28 * MIB),
        cost_estimate=pl.CostEstimate(flops=25_000_000_000 * (end - first), bytes_accessed=10_000_000, transcendentals=0),
    )(*tables, queries, grad_rows, attended, totals, keys, values)


def xor_send(array, axis, bit):
    size = lax.axis_size(axis)
    return lax.ppermute(array, axis, [(i, i ^ bit) for i in range(size)])


def shift_send(array, shift):
    size = lax.axis_size("ka")
    return lax.ppermute(array, "ka", [(i, (i + shift) % size) for i in range(size)])


def pick(array, index, axis=0):
    return lax.dynamic_index_in_dim(array, index, axis, keepdims=False)


def rows_at(array, index):
    return array.at[index].get(mode="promise_in_bounds")


def together(value, *others):
    return lax.optimization_barrier((value,) + others)[0]


def member_send(array, offset):
    if offset & 1:
        array = xor_send(array, "pb", 1)
    if offset >> 1:
        array = xor_send(array, "ka", offset >> 1)
    return array


def share_with_group(array, members):
    return jnp.concatenate([array] + [member_send(array, e) for e in range(1, members)], axis=0)


def plan_kernel(members, long, keys, me, held_piece, order, bounds, place, rank, by_rank, held):
    count = 4 * members

    def extremes(p, seen):
        return jnp.minimum(seen[0], keys[p]), jnp.maximum(seen[1], keys[p])

    least, most = lax.fori_loop(0, count, extremes, (keys[0], keys[0]))
    short = most - least >= long
    size = jnp.where(short, members // 2, members)

    def rank_one(p, _):
        r = lax.fori_loop(
            0, count, lambda q, r: r + jnp.where(keys[q] < keys[p], 1, 0), jnp.int32(0)
        )
        rank[p] = r
        by_rank[r] = p
        return 0

    lax.fori_loop(0, count, rank_one, 0)
    for e in range(members):
        member = me[0] ^ e
        second = jnp.where(short & (member >= members // 2), 1, 0)
        number = member - second * (members // 2)
        base = second * (2 * members)
        spread = (number, 2 * size - 1 - number, 2 * size + number, 4 * size - 1 - number)
        for i, r in enumerate(spread):
            held[4 * e + i] = base + r
            order[base + r] = 4 * e + i
            held_piece[4 * e + i] = by_rank[base + r]
            if e == 0:
                bounds[i] = base
                bounds[4 + i] = base + r

    def place_one(p, _):
        place[p] = order[rank[p]]
        return 0

    lax.fori_loop(0, count, place_one, 0)


def plan(keys, member, members, long):
    count = 4 * members
    smem = pl.BlockSpec(memory_space=pltpu.SMEM)
    table = jax.ShapeDtypeStruct((count,), jnp.int32)
    return pl.pallas_call(
        functools.partial(plan_kernel, members, long),
        out_shape=(table, table, jax.ShapeDtypeStruct((2 * OWN,), jnp.int32), table),
        in_specs=[smem, smem],
        out_specs=[smem] * 4,
        scratch_shapes=[pltpu.SMEM((count,), jnp.int32)] * 3,
    )(keys, jnp.reshape(member, (1,)).astype(jnp.int32))


class Layout:
    def __init__(self, sequence_ids, sequence_offsets):
        self.core = lax.axis_index("pb") % 2
        self.z = lax.axis_index("ka")
        self.depth = lax.axis_size("ka")
        self.subs = self.depth // 4
        self.members = self.depth // 2
        tall = sequence_ids.shape[0]
        self.rows = tall // OWN
        self.long = tall // BATCH * self.depth
        keys = (sequence_ids * self.long + sequence_offsets).reshape(OWN, self.rows)[:, :1]
        self.keys_under_way = self.send_in(
            jnp.broadcast_to(keys, (OWN, self.subs)).reshape(-1)
        )

    def settle(self):
        keys = self.arrived(self.keys_under_way).reshape(-1, self.subs)[:, 0]
        member = (self.z % self.subs) * 2 + self.core
        self.held_piece, self.order, self.bounds, self.place = plan(
            keys, member, self.members, self.long
        )
        self.tables = (self.bounds, self.order)

    def bits(self, place):
        return place // (2 * self.subs), place // self.subs % 2, place % self.subs

    def round_pairs(self, turn):
        pairs = []
        for pb in range(lax.axis_size("pb")):
            for z in range(self.depth):
                half, batch, sub = (a ^ b for a, b in zip(self.bits(z), self.bits(turn)))
                target = (2 * (pb % 2) + batch) * self.subs + sub
                pairs.append((pb * self.depth + z, (pb // 2 * 2 + half) * self.depth + target))
        return pairs

    def send_in(self, array):
        part_rows = array.shape[0] // (OWN * self.subs)
        blocks = array.reshape((BATCH, HALVES, self.subs, part_rows) + array.shape[1:])
        parts = []
        for turn in range(self.depth):
            half, batch, sub = (a ^ b for a, b in zip(self.bits(self.z), self.bits(turn)))
            part = pick(pick(pick(blocks, batch), half), sub)
            parts.append(lax.ppermute(part, ("pb", "ka"), self.round_pairs(turn)))
        return parts

    def arrived(self, parts):
        if self.subs == 1:
            return jnp.concatenate(parts + [xor_send(part, "pb", 1) for part in parts])
        held = jnp.concatenate(parts)
        part_rows, trailing = parts[0].shape[0], parts[0].shape[1:]
        held = held.reshape((4, self.subs, part_rows) + trailing)
        held = jnp.take(held, self.z % self.subs ^ jnp.arange(self.subs), axis=1)
        quarters = [[g * self.subs + i for i in range(self.subs)] for g in range(4)]
        held = lax.all_gather(held, "ka", axis=2, axis_index_groups=quarters)
        held = held.reshape((4 * self.subs * self.subs * part_rows,) + trailing)
        return jnp.concatenate([held, xor_send(held, "pb", 1)])


class Moving:
    def advance(self, value):
        self.launch(self.prepare(value))


class ScatterOut(Moving):
    def __init__(self, own, layout):
        self.layout = layout
        self.steps = ["first", "second", "assemble"]
        self.result = share_with_group(own, layout.members)

    def prepare(self, value):
        self.now = self.steps.pop(0) if self.steps else None
        turns = self.layout.depth // 2
        if self.now == "first":
            parts = self.parts(value)
            return parts[:turns], parts[turns:]
        return self.assemble(sum(value, [])) if self.now == "assemble" else value

    def launch(self, value):
        turns = self.layout.depth // 2
        if self.now == "first":
            value = (self.send(value[0], 0), value[1])
        elif self.now == "second":
            value = (value[0], self.send(value[1], turns))
        self.result = value

    def send(self, parts, first):
        return [
            lax.ppermute(part, ("pb", "ka"), [(b, a) for a, b in self.layout.round_pairs(turn)])
            for turn, part in enumerate(parts, first)
        ]

    def parts(self, shared):
        layout = self.layout
        subs = layout.subs
        rows, width = shared.shape[1:]
        shared = shared.reshape(-1, subs, rows // subs, width)
        sub = layout.z % subs
        parts = []
        for turn in range(layout.depth):
            piece = turn if subs == 1 else turn // subs * subs + (sub ^ turn % subs)
            parts.append(pick(pick(shared, pick(layout.place, piece)), sub))
        return parts

    def assemble(self, got):
        layout = self.layout
        subs = layout.subs
        order = []
        for block in range(OWN * subs):
            batch, half, part = block // (2 * subs), block // subs % 2, block % subs
            z_half, z_batch, z_sub = layout.bits(layout.z)
            order.append(((z_half ^ half) * 2 + (z_batch ^ batch)) * subs + (z_sub ^ part))
        return rows_at(jnp.stack(got), jnp.stack(order)).reshape(-1, got[0].shape[-1])


class VectorSum(Moving):
    def __init__(self, vectors):
        self.sizes = [v.shape[0] for v in vectors]
        self.steps = []
        for axis in ("ka", "pb"):
            bits = lax.axis_size(axis).bit_length() - 1
            self.steps += [(axis, 1 << b) for b in range(bits)]
        self.advance(jnp.concatenate(vectors).reshape(-1, 128))

    def prepare(self, flat):
        self.now = self.steps.pop(0) if self.steps else None
        return flat

    def launch(self, flat):
        self.result = flat + xor_send(flat, *self.now) if self.now else flat

    def parts(self):
        flat, at, result = self.result.reshape(-1), 0, []
        for size in self.sizes:
            result.append(flat[at : at + size])
            at += size
        return result


class BundleSum(Moving):
    def __init__(self, arrays, segments):
        self.along_pb, self.along_ka = lax.axis_size("pb"), lax.axis_size("ka")
        self.bits = self.along_pb.bit_length() - 1
        rest = list(range(1, self.bits))
        self.steps = list(zip(rest, rest[::-1])) + ["ka"]
        self.narrow = arrays[0][0].shape[-1]
        self.segments = segments
        self.result = []
        for kept, sent in arrays:
            total = kept + xor_send(sent, "pb", 1)
            self.result.append(total.reshape((2,) * (self.bits - 1) + (1,) + kept.shape[1:]))

    def split(self, view, bit):
        axis = self.bits - 1 - bit
        own = (lax.axis_index("pb") >> bit) & 1
        kept = lax.dynamic_slice_in_dim(view, own, 1, axis)
        return kept, lax.dynamic_slice_in_dim(view, 1 - own, 1, axis)

    def prepare(self, views):
        self.now = self.steps.pop(0) if self.steps else None
        if not self.now:
            return views
        if self.now != "ka":
            if len(views) == 1:
                half = views[0].shape[-2] // 2
                views = [views[0][..., :half, :], views[0][..., half:, :]]
            return [self.split(view, bit) for view, bit in zip(views, self.now)]
        return split_columns(
            [v.reshape(-1, self.narrow) for v in views], self.segments, self.along_ka
        )

    def launch(self, made):
        if not self.now:
            self.result = made
        elif self.now != "ka":
            self.result = [
                kept + xor_send(sent, "pb", 1 << bit)
                for (kept, sent), bit in zip(made, self.now)
            ]
        else:
            got = [shift_send(sent, shift) for shift, sent in enumerate(made[1:], 1)]
            self.result = [made[0]] + got

    def matrices(self):
        return join_columns(self.result, self.segments, self.narrow, self.along_ka)


def split_kernel(segments, ways, z, *refs):
    views, outs, whole = refs[:-ways - 1], refs[-ways - 1 : -1], refs[-1]
    at = 0
    for view in views:
        whole[at : at + view.shape[0], :] = view[...]
        at += view.shape[0]
    narrow = whole.shape[1]
    thin = narrow // ways
    for target in range(ways):
        pieces, at = [], 0
        for height, folds in segments:
            share = ways // folds
            first = at + target // share * height
            wide = narrow // share
            for i in range(wide // thin):
                left = target % share * wide + i * thin
                pieces.append(whole[first : first + height, left : left + thin])
            at += height * folds
        rows = jnp.concatenate(pieces, axis=0)
        half = rows.shape[0] // 2
        block = jnp.concatenate([rows[:half], rows[half:]], axis=1)
        for shift in range(ways):

            @pl.when((z[0] + shift) % ways == target)
            def _():
                outs[shift][...] = block


def split_columns(views, segments, ways):
    narrow = views[0].shape[1]
    height = sum(v.shape[0] for v in views)
    shape = jax.ShapeDtypeStruct((height // 2, 2 * narrow // ways), BF)
    vmem = pl.BlockSpec(memory_space=pltpu.VMEM)
    return pl.pallas_call(
        functools.partial(split_kernel, segments, ways),
        out_shape=[shape] * ways,
        in_specs=[pl.BlockSpec(memory_space=pltpu.SMEM)] + [vmem] * len(views),
        out_specs=[vmem] * ways,
        scratch_shapes=[pltpu.VMEM((height, narrow), BF)],
        compiler_params=pltpu.CompilerParams(vmem_limit_bytes=16 * MIB),
    )(lax.axis_index("ka").reshape(1).astype(jnp.int32), *views)


def join_kernel(segments, narrow, ways, *refs):
    parts, outs = refs[:ways], refs[ways:]
    total = parts[0][...].astype(F32)
    for part in parts[1:]:
        total = total + part[...].astype(F32)
    thin = narrow // ways
    rows = jnp.concatenate([total[:, :thin], total[:, thin:]], axis=0)
    at = 0
    for (height, folds), out in zip(segments, outs):
        pieces = [rows[at + i * height : at + (i + 1) * height] for i in range(folds)]
        out[...] = pieces[0] if folds == 1 else jnp.concatenate(pieces, axis=1)
        at += height * folds


def join_columns(parts, segments, narrow, ways):
    vmem = pl.BlockSpec(memory_space=pltpu.VMEM)
    thin = narrow // ways
    return pl.pallas_call(
        functools.partial(join_kernel, segments, narrow, ways),
        out_shape=[jax.ShapeDtypeStruct((height, thin * folds), F32) for height, folds in segments],
        in_specs=[vmem] * ways,
        out_specs=[vmem] * len(segments),
        compiler_params=pltpu.CompilerParams(vmem_limit_bytes=16 * MIB),
    )(*parts)


class Background:
    def __init__(self):
        self.moving = []

    def tick(self, value):
        live = [m for m in self.moving if not getattr(m, "ended", False)]
        value, results = lax.optimization_barrier((value, [m.result for m in live]))
        for m in live:
            m.ended = not m.steps
        made = [m.prepare(r) for m, r in zip(live, results)]
        value, made = lax.optimization_barrier((value, made))
        for m, parts in zip(live, made):
            m.launch(parts)
        return value

    def drain(self):
        for m in self.moving:
            while m.steps:
                m.advance(m.result)


def normalized(values):
    centre = values - jnp.mean(values, axis=-1, keepdims=True)
    spread = jnp.mean(centre * centre, axis=-1, keepdims=True)
    scale = lax.rsqrt(spread + EPSILON)
    return centre * scale, scale


def layer_norm(values, gain, shift):
    return (normalized(values)[0] * gain.astype(F32) + shift.astype(F32)).astype(BF)


def norm_backward(values, gain, upstream):
    n, scale = normalized(values)
    grad_gain = jnp.sum(upstream * n, axis=0)
    grad_shift = jnp.sum(upstream, axis=0)
    dn = upstream * gain.astype(F32)
    mean = jnp.mean(dn, axis=-1, keepdims=True)
    along = jnp.mean(dn * n, axis=-1, keepdims=True)
    return scale * (dn - mean - n * along), grad_gain, grad_shift


def gelu_pair(u):
    size = jnp.abs(u) * 0.7071067811865476
    t = 1.0 / (1.0 + 0.3275911 * size)
    bell = jnp.exp(-0.5 * u * u)
    series = t * (
        0.254829592
        + t * (-0.284496736 + t * (1.421413741 + t * (-1.453152027 + t * 1.061405429)))
    )
    tail = 0.5 * series * bell
    phi = jnp.where(u < 0, tail, 1.0 - tail)
    return u * phi, phi + u * (bell * 0.3989422804014327)


def row_tiles(tall):
    tile = min(256, tall)
    return [slice(r, r + tile) for r in range(0, tall, tile)]


def norm_rows(values, gain, shift):
    centre = values - jnp.mean(values, axis=-1, keepdims=True)
    spread = jnp.mean(centre * centre, axis=-1, keepdims=True)
    return (centre * lax.rsqrt(spread + EPSILON) * gain + shift).astype(BF)


def mlp_kernel(
    following, o_ref, x_ref, wo_ref, gain_ref, bias_ref, wu_ref, ub_ref, wd_ref, db_ref, ng_ref, nb_ref,
    x1_ref, h2_ref, a_ref, s_ref, y_ref, *rest,
):
    acc = rest[-1]
    step = pl.program_id(0)
    tiles = row_tiles(o_ref.shape[0])

    @pl.when(step == 0)
    def _():
        gain, shift = gain_ref[...].astype(F32), bias_ref[...].astype(F32)
        for t in tiles:
            x1 = x_ref[t].astype(F32) + dot(o_ref[t], wo_ref[...])
            x1_ref[t] = x1
            h2_ref[t] = norm_rows(x1, gain, shift)
            acc[t] = jnp.zeros_like(x1)

    up_bias = ub_ref[...].astype(F32)
    for t in tiles:
        u = dot(h2_ref[t], wu_ref[...]) + up_bias
        active, slope = gelu_pair(u)
        active = active.astype(BF)
        a_ref[t] = active
        s_ref[t] = slope.astype(BF)
        acc[t] += dot(active, wd_ref[...])

    @pl.when(step == pl.num_programs(0) - 1)
    def _():
        down_bias = db_ref[...].astype(F32)
        gain, shift = ng_ref[...].astype(F32), nb_ref[...].astype(F32)
        for t in tiles:
            y = x1_ref[t] + (acc[t] + down_bias)
            y_ref[t] = y.astype(y_ref.dtype)
            if following:
                rest[0][t] = norm_rows(y, gain, shift)


ONCE = pl.Buffered(1)


def whole_block(array):
    return pl.BlockSpec(array.shape, lambda i: (0,) * len(array.shape), pipeline_mode=ONCE)


def cost(flops, *arrays):
    moved = sum(a.size * a.dtype.itemsize for a in arrays)
    return pl.CostEstimate(flops=flops, bytes_accessed=moved, transcendentals=0)


def mlp_forward(attended, x_own, params, following):
    (_, _, _, _, _, w_out, mlp_gain, mlp_bias, w_up, up_bias, w_down, down_bias) = params
    tall, width = attended.shape
    hidden = w_up.shape[1]
    row = lambda v: v.reshape(1, -1)
    gain, shift = following or (mlp_gain, mlp_bias)
    inputs = (
        attended, x_own, w_out, row(mlp_gain), row(mlp_bias), w_up, row(up_bias), w_down,
        row(down_bias), row(gain), row(shift),
    )
    specs = [whole_block(a) for a in inputs]
    specs[5] = pl.BlockSpec((width, width), lambda i: (0, i))
    specs[6] = pl.BlockSpec((1, width), lambda i: (0, i))
    specs[7] = pl.BlockSpec((width, width), lambda i: (i, 0))
    wide, narrow = (tall, hidden), (tall, width)
    shapes = [(narrow, F32), (narrow, BF), (wide, BF), (wide, BF), (narrow, F32 if following else BF)]
    shapes += [(narrow, BF)] if following else []
    out_shape = [jax.ShapeDtypeStruct(shape, kind) for shape, kind in shapes]
    chunk = pl.BlockSpec((tall, width), lambda i: (0, i))
    full = pl.BlockSpec((tall, width), lambda i: (0, 0), pipeline_mode=ONCE)
    return pl.pallas_call(
        functools.partial(mlp_kernel, following is not None),
        out_shape=out_shape,
        grid=(hidden // width,),
        in_specs=specs,
        out_specs=[full, full, chunk, chunk, full] + ([full] if following else []),
        scratch_shapes=[pltpu.VMEM((tall, width), F32)],
        compiler_params=pltpu.CompilerParams(vmem_limit_bytes=36 * MIB),
        cost_estimate=cost(2 * tall * width * (2 * hidden + width), *inputs, *out_shape),
    )(*inputs)


def mlp_back_kernel(
    g_ref, slope_ref, wd_ref, wu_ref, x1_ref, gain_ref, wo_ref,
    du_ref, dx_ref, gx_ref, do_ref, gb_ref, sums_ref, vectors_ref, acc,
):
    step = pl.program_id(0)
    tiles = row_tiles(g_ref.shape[0])

    @pl.when(step == 0)
    def _():
        for t in tiles:
            gb_ref[t] = g_ref[t].astype(BF)
            acc[t] = jnp.zeros(acc[t].shape, F32)

    total = 0.0
    for t in tiles:
        da = dot(gb_ref[t], wd_ref[...], NT)
        du = (da * slope_ref[t].astype(F32)).astype(BF)
        du_ref[t] = du
        total = total + jnp.sum(du.astype(F32), axis=0, keepdims=True)
        acc[t] += dot(du, wu_ref[...], NT)
    sums_ref[...] = total

    @pl.when(step == pl.num_programs(0) - 1)
    def _():
        gain = gain_ref[...].astype(F32)
        of_gain = of_shift = of_down = 0.0
        for t in tiles:
            dh2, x1 = acc[t], x1_ref[t]
            centre = x1 - jnp.mean(x1, axis=-1, keepdims=True)
            scale = lax.rsqrt(jnp.mean(centre * centre, axis=-1, keepdims=True) + EPSILON)
            n = centre * scale
            of_gain = of_gain + jnp.sum(dh2 * n, axis=0, keepdims=True)
            of_shift = of_shift + jnp.sum(dh2, axis=0, keepdims=True)
            of_down = of_down + jnp.sum(gb_ref[t].astype(F32), axis=0, keepdims=True)
            dn = dh2 * gain
            mean = jnp.mean(dn, axis=-1, keepdims=True)
            along = jnp.mean(dn * n, axis=-1, keepdims=True)
            dx = g_ref[t].astype(F32) + scale * (dn - mean - n * along)
            dx_ref[t] = dx
            gx = dx.astype(BF)
            gx_ref[t] = gx
            do_ref[t] = dot(gx, wo_ref[...], NT).astype(BF)
        vectors_ref[0:1, :] = of_gain
        vectors_ref[1:2, :] = of_shift
        vectors_ref[2:3, :] = of_down


def mlp_backward(upstream, slope, middle, params):
    (_, _, _, _, _, w_out, mlp_gain, _, w_up, _, w_down, _) = params
    tall, width = upstream.shape
    hidden = slope.shape[1]
    inputs = (upstream, slope, w_down, w_up, middle, mlp_gain.reshape(1, -1), w_out)
    specs = [whole_block(a) for a in inputs]
    specs[1] = pl.BlockSpec((tall, width), lambda i: (0, i))
    specs[2] = pl.BlockSpec((width, width), lambda i: (i, 0))
    specs[3] = pl.BlockSpec((width, width), lambda i: (0, i))
    shapes = [((tall, hidden), BF), ((tall, width), F32)] + [((tall, width), BF)] * 3
    shapes += [((1, hidden), F32), ((3, width), F32)]
    out_shape = [jax.ShapeDtypeStruct(shape, kind) for shape, kind in shapes]
    full = pl.BlockSpec((tall, width), lambda i: (0, 0), pipeline_mode=ONCE)
    return pl.pallas_call(
        mlp_back_kernel,
        out_shape=out_shape,
        grid=(hidden // width,),
        in_specs=specs,
        out_specs=[
            pl.BlockSpec((tall, width), lambda i: (0, i)), full, full, full, full,
            pl.BlockSpec((1, width), lambda i: (0, i)), pl.BlockSpec((3, width), lambda i: (0, 0)),
        ],
        scratch_shapes=[pltpu.VMEM((tall, width), F32)],
        compiler_params=pltpu.CompilerParams(vmem_limit_bytes=40 * MIB),
        cost_estimate=cost(2 * tall * width * (2 * hidden + width), *inputs, *out_shape),
    )(*inputs)


def put_halves(core, kept_ref, sent_ref, low, high):
    @pl.when(core == 0)
    def _():
        kept_ref[...] = low
        sent_ref[...] = high

    @pl.when(core != 0)
    def _():
        kept_ref[...] = high
        sent_ref[...] = low


def by_blocks(product, blocks):
    height, breadth = product.shape
    parts = product.astype(BF).reshape(blocks // 2, 2, height // blocks, breadth)
    return parts[:, 0], parts[:, 1]


def mlp_weights_kernel(
    blocks, folds, core, h2_ref, du_ref, o_ref, gx_ref, a_ref, gb_ref,
    kept_a, sent_a, kept_b, sent_b,
):
    step = pl.program_id(0)

    @pl.when(step < folds)
    def _():
        put_halves(core[0], kept_a, sent_a, *by_blocks(dot(h2_ref[...], du_ref[...], TN), blocks))

    @pl.when(step == folds)
    def _():
        put_halves(core[0], kept_a, sent_a, *by_blocks(dot(o_ref[...], gx_ref[...], TN), blocks))

    @pl.when(step > folds)
    def _():
        product = dot(a_ref[...], gb_ref[...], TN)
        pairs, _, height, _ = kept_b.shape
        parts = product.astype(BF).reshape(pairs, 1, 2, height, product.shape[1])
        put_halves(core[0], kept_b, sent_b, parts[:, :, 0], parts[:, :, 1])


def mlp_weights(h2, du, attended, gx, active, gb):
    blocks = lax.axis_size("pb")
    tall, width = h2.shape
    hidden = du.shape[1]
    folds = hidden // width
    thin, tall_block = width // blocks, hidden // blocks
    pairs = blocks // 2 // folds
    full = pl.BlockSpec((tall, width), lambda i, c: (0, 0), pipeline_mode=ONCE)
    a_block = pl.BlockSpec(
        (blocks // 2, thin, width), lambda i, c: (0, jnp.minimum(i, folds), 0)
    )
    b_block = pl.BlockSpec(
        (pairs, 1, tall_block, width), lambda i, c: (jnp.maximum(i - folds - 1, 0), 0, 0, 0)
    )
    a_shape = jax.ShapeDtypeStruct((blocks // 2, thin * (folds + 1), width), BF)
    b_shape = jax.ShapeDtypeStruct((blocks // 2, 1, tall_block, width), BF)
    core = (lax.axis_index("pb") % 2).reshape(1).astype(jnp.int32)
    inputs = (h2, du, attended, gx, active, gb)
    kept_a, sent_a, kept_b, sent_b = pl.pallas_call(
        functools.partial(mlp_weights_kernel, blocks, folds),
        out_shape=(a_shape, a_shape, b_shape, b_shape),
        grid_spec=pltpu.PrefetchScalarGridSpec(
            num_scalar_prefetch=1,
            grid=(2 * folds + 1,),
            in_specs=[
                full,
                pl.BlockSpec((tall, width), lambda i, c: (0, jnp.minimum(i, folds - 1))),
                full,
                full,
                pl.BlockSpec((tall, width), lambda i, c: (0, jnp.clip(i - folds - 1, 0, folds - 1))),
                full,
            ],
            out_specs=[a_block, a_block, b_block, b_block],
        ),
        compiler_params=pltpu.CompilerParams(vmem_limit_bytes=32 * MIB),
        cost_estimate=cost(2 * tall * width * (2 * hidden + width), *inputs, a_shape, b_shape),
    )(core, *inputs)
    flat = lambda v: v.reshape(blocks // 2, tall_block, width)
    arrays = [(kept_a, sent_a), (flat(kept_b), flat(sent_b))]
    return BundleSum(arrays, [(thin, folds), (thin, 1), (tall_block, 1)])


def attention_weights_kernel(blocks, core, *refs):
    h_ref, kept_ref, sent_ref = refs[0], refs[-2], refs[-1]
    parts = refs[1:-2]
    count = len(parts) // 3
    for which in range(3):

        @pl.when(pl.program_id(0) == which)
        def _():
            products = [
                dot(h_ref[: part.shape[0], :], part[...], TN)
                for part in parts[which * count : (which + 1) * count]
            ]
            product = products[0] if count == 1 else jnp.concatenate(products, axis=1)
            put_halves(core[0], kept_ref, sent_ref, *by_blocks(product, blocks))


def attention_weights(h_all, dqs, dks, dvs):
    blocks = lax.axis_size("pb")
    width = h_all.shape[1]
    thin = width // blocks
    inputs = (h_all, *dqs, *dks, *dvs)
    block = pl.BlockSpec((blocks // 2, thin, width), lambda i, c: (0, i, 0))
    shape = jax.ShapeDtypeStruct((blocks // 2, 3 * thin, width), BF)
    core = (lax.axis_index("pb") % 2).reshape(1).astype(jnp.int32)
    kept, sent = pl.pallas_call(
        functools.partial(attention_weights_kernel, blocks),
        out_shape=(shape, shape),
        grid_spec=pltpu.PrefetchScalarGridSpec(
            num_scalar_prefetch=1,
            grid=(3,),
            in_specs=[
                pl.BlockSpec(a.shape, lambda i, c: (0, 0), pipeline_mode=ONCE) for a in inputs
            ],
            out_specs=[block, block],
        ),
        compiler_params=pltpu.CompilerParams(vmem_limit_bytes=28 * MIB),
        cost_estimate=cost(5 * h_all.shape[0] * width * width, *inputs, shape),
    )(core, *inputs)
    return BundleSum([(kept, sent)], [(thin, 1)] * 3)


def layer_forward(x_own, h_all, params, layout, signed, passing, following):
    (_, _, w_query, w_key, w_value, *_) = params
    tall, width = x_own.shape
    rows = layout.rows
    scale = (width // HEADS) ** -0.5
    queries = (dense(h_all[:tall], w_query, 1, 0) * scale).astype(BF).reshape(OWN, rows, width)
    keys = dense(h_all, w_key, 1, 0).astype(BF).reshape(-1, rows, width)
    values = dense(h_all, w_value, 1, 0).astype(BF).reshape(-1, rows, width)
    attended, totals = attend_forward(queries, keys, values, layout.tables, signed)
    (attended, totals), passing = lax.optimization_barrier(((attended, totals), passing))
    middle, h2, active, slope, *result = mlp_forward(
        attended.reshape(tall, width), x_own, params, following
    )
    saved = (h_all, queries, keys, values, attended, totals, middle, h2, active, slope)
    return result, saved, passing


def layer_backward(upstream, x_own, params, saved, layout, signed, background, cuts, earlier):
    (norm_gain, _, w_query, w_key, w_value, *_) = params
    h_all, queries, keys, values, attended, totals, middle, h2, active, slope = saved
    tall, width = x_own.shape
    du, dx1, gx, do, gb, sum_du, vectors = mlp_backward(upstream, slope, middle, params)
    mlp_vectors = (vectors[0], vectors[1], sum_du[0], vectors[2])
    sum_mlp = mlp_weights(h2, du, attended.reshape(tall, width), gx, active, gb)
    background.moving.append(sum_mlp)
    sum_vectors = VectorSum(earlier + mlp_vectors) if earlier else None
    if earlier:
        background.moving.append(sum_vectors)
    do = do.reshape(queries.shape)
    outcome = []
    for first, end in zip(cuts, cuts[1:]):
        do = background.tick(do)
        if end > first:
            outcome.append(
                attend_backward(
                    queries, do, attended, totals, keys, values, layout.tables, signed, first, end
                )
            )
            do = together(do, outcome[-1])
    outcome = background.tick(outcome)
    dqs, dks, dvs = ([p.reshape(-1, p.shape[-1]) for p in parts] for parts in zip(*outcome))
    dq, dk, dv = (jnp.concatenate(parts, axis=-1) for parts in (dqs, dks, dvs))
    from_keys = (dense(dk, w_key, 1, 1) + dense(dv, w_value, 1, 1)).astype(BF)
    (dqs, dks, dvs), from_keys = lax.optimization_barrier(((dqs, dks, dvs), from_keys))
    from_keys = from_keys.reshape(layout.members, tall, width)
    given = [member_send(from_keys[e], e) for e in range(1, layout.members)]
    dh = dense(dq, w_query, 1, 1) + from_keys[0].astype(F32)
    sum_att = attention_weights(h_all, dqs, dks, dvs)
    background.moving.append(sum_att)
    for part in given:
        dh = dh + part.astype(F32)
    dx, grad_norm_gain, grad_norm_bias = norm_backward(x_own.astype(F32), norm_gain, dh)
    norm_vectors = (grad_norm_gain, grad_norm_bias)

    def finish(mlp, norm):
        up, out, down = sum_mlp.matrices()
        query, key, value = sum_att.matrices()
        return (
            norm[0], norm[1], query, key, value, out,
            mlp[0], mlp[1], up, mlp[2], down, mlp[3],
        )

    return dx1 + dx, mlp_vectors, norm_vectors, sum_vectors, finish


def per_device(tokens, sequence_ids, sequence_offsets, *rest):
    signed_params, plain_params, cotangent = rest[:12], rest[12:24], rest[24]
    tall, width = tokens.shape
    layout = Layout(sequence_ids, sequence_offsets)
    tokens, layout.keys_under_way = lax.optimization_barrier((tokens, layout.keys_under_way))
    rows = layout.rows
    background = Background()
    x_all = layout.arrived(layout.send_in(tokens)).reshape(-1, rows, width)
    layout.settle()
    x_held = rows_at(x_all, layout.held_piece).reshape(-1, width)
    cotangent = layout.send_in(together(cotangent, x_held))
    h_all = layer_norm(x_held.astype(F32), signed_params[0], signed_params[1])
    x_own = x_held[:tall]
    (between, h_own), signed_saved, cotangent = layer_forward(
        x_own, h_all, signed_params, layout, True, cotangent, plain_params[:2]
    )
    h_all = share_with_group(h_own, layout.members)
    upstream = layout.arrived(cotangent).reshape(-1, rows, width)
    (final,), plain_saved, upstream = layer_forward(
        between, h_all, plain_params, layout, False, upstream, None
    )
    output = ScatterOut(final.reshape(OWN, rows, width), layout)
    background.moving.append(output)
    upstream = rows_at(upstream, layout.held_piece[:OWN]).reshape(tall, width)
    groups = attention_sizes(width)[2]
    upstream, mlp_plain, norm_plain, _, finish_plain = layer_backward(
        upstream, between, plain_params, plain_saved, layout, False, background,
        (0, max(1, groups * 2 // 3), groups), (),
    )
    upstream = background.tick(upstream)
    upstream, _, norm_signed, early, finish_signed = layer_backward(
        upstream, x_own, signed_params, signed_saved, layout, True, background,
        tuple(range(groups + 1)), mlp_plain + norm_plain,
    )
    upstream = background.tick(upstream)
    back = ScatterOut(upstream.astype(BF).reshape(OWN, rows, width), layout)
    late = VectorSum(norm_signed)
    background.moving += [back, late]
    background.tick(())
    background.drain()
    early, late = early.parts(), late.parts()
    return (
        (output.result, back.result.astype(F32))
        + finish_signed(early[6:], late)
        + finish_plain(early[:4], early[4:6])
    )


def solution(mesh):
    rows, block = P(("pb", "ka"), None), P("pb", "ka")
    grads = (P(), P(), block, block, block, block, P(), P(), block, P(), block, P())
    return jax.shard_map(
        per_device,
        mesh=mesh,
        in_specs=(rows, P(("pb", "ka")), P(("pb", "ka"))) + (P(),) * 24 + (rows,),
        out_specs=(rows, rows) + grads + grads,
        check_vma=False,
    )
```

```python
import functools

import jax
import jax.numpy as jnp
from jax import lax
from jax.experimental import pallas as pl
from jax.experimental.pallas import tpu as pltpu
from jax.sharding import PartitionSpec as P

HEADS = 12
BATCH = 2
HALVES = 2
OWN = BATCH * HALVES
EPSILON = 1e-05
FLOOR = -1e30
LEAST, MOST = 1e-25, 1e30
BF = jnp.bfloat16
F32 = jnp.float32
MIB = 1 << 20

NT = (((1,), (1,)), ((), ()))
NN = (((1,), (0,)), ((), ()))
TN = (((0,), (0,)), ((), ()))


def dot(left, right, dims=NN):
    return lax.dot_general(left, right, dims, preferred_element_type=F32)


def dense(left, right, left_axis, right_axis):
    return lax.dot_general(
        left, right, (((left_axis,), (right_axis,)), ((), ())), preferred_element_type=F32
    )


def attention_sizes(width):
    head = width // HEADS
    lanes = 256
    while width % lanes or lanes % head:
        lanes //= 2
    return head, lanes, width // lanes, lanes // head


def head_parts(block, head, count):
    tile = min(128, block.shape[1])
    per = tile // head
    lane = lax.broadcasted_iota(jnp.int32, (block.shape[0], tile), 1) // head
    tiles = [block[:, t : t + tile] for t in range(0, block.shape[1], tile)]
    zero = jnp.zeros_like(tiles[0])
    return [jnp.where(lane == h % per, tiles[h // per], zero) for h in range(count)]


def tiles_of(block, head, count):
    tile = min(128, block.shape[1])
    per = tile // head
    tiles = [block[:, t : t + tile] for t in range(0, block.shape[1], tile)]
    return [tiles[h // per] for h in range(count)]


def join_tiles(parts, head):
    per = parts[0].shape[1] // head
    sums = [sum(parts[h + 1 : h + per], parts[h]) for h in range(0, len(parts), per)]
    return sums[0] if len(sums) == 1 else jnp.concatenate(sums, axis=1)


def turned(block):
    return jnp.transpose(block.astype(F32))


def causal(shape):
    key = lax.broadcasted_iota(jnp.int32, shape, 0)
    query = lax.broadcasted_iota(jnp.int32, shape, 1)
    return key <= query


def forward_kernel(head, count, signed, bounds, order, q_ref, k_ref, v_ref, o_ref, lse_ref, qm, vt, acc, sums):
    step = pl.program_id(1)

    @pl.when(step == 0)
    def _():
        for j in range(k_ref.shape[0]):
            vt[j] = turned(v_ref[j]).astype(BF)

    for h, part in enumerate(head_parts(q_ref[0], head, count)):
        qm[h] = part
    rows = q_ref.shape[1]
    start, last = bounds[step], bounds[OWN + step]

    def scores(j):
        return [dot(keys, qm[h], NT) for h, keys in enumerate(tiles_of(k_ref[j], head, count))]

    def magnitude(s, masked):
        c, ratio = s, None
        if signed:
            square = s * s + 1.0
            inverse = lax.rsqrt(square)
            c, ratio = square * inverse, s * inverse
        if masked:
            c = jnp.where(causal(c.shape), c, FLOOR)
        return c, ratio

    def weigh(j, h, raised, ratio):
        if signed:
            raised = raised * ratio
        return dot(vt[j, h * head : (h + 1) * head, :], raised.astype(BF))

    def plain_block(j, carry, masked):
        result = []
        for h, s in enumerate(scores(j)):
            c, ratio = magnitude(s, masked)
            raised = jnp.exp(c)
            result.append(carry[h] + jnp.sum(raised, axis=0, keepdims=True))
            acc[h] += weigh(j, h, raised, ratio)
        return tuple(result)

    def safe_block(j, carry, masked):
        result = []
        for h, s in enumerate(scores(j)):
            top, total = carry[2 * h], carry[2 * h + 1]
            c, ratio = magnitude(s, masked)
            higher = jnp.maximum(top, jnp.max(c, axis=0, keepdims=True))
            raised = jnp.exp(c - higher)
            fade = jnp.exp(top - higher)
            acc[h] = acc[h] * fade + weigh(j, h, raised, ratio)
            result += [higher, total * fade + jnp.sum(raised, axis=0, keepdims=True)]
        return tuple(result)

    def over_keys(block, first):
        acc[...] = jnp.zeros_like(acc)
        carry = lax.fori_loop(start, last, lambda j, c: block(order[j], c, False), first)
        return block(step, carry, True)

    zeros = jnp.zeros((1, rows), F32)
    totals = jnp.concatenate(over_keys(plain_block, (zeros,) * count), axis=0)
    fine = jnp.min(jnp.where((totals > LEAST) & (totals < MOST), 1.0, 0.0)) > 0.5
    sums[...] = totals
    lse_ref[0] = jnp.log(totals)

    @pl.when(jnp.logical_not(fine))
    def _():
        carry = over_keys(safe_block, (zeros + FLOOR, zeros) * count)
        for h in range(count):
            sums[h : h + 1, :] = carry[2 * h + 1]
            lse_ref[0, h : h + 1, :] = carry[2 * h] + jnp.log(carry[2 * h + 1])

    share = 1.0 / sums[...]
    for h in range(count):
        acc[h] = acc[h] * share[h : h + 1, :]
    o_ref[0] = jnp.transpose(acc[...].reshape(count * head, rows)).astype(BF)


def attend_forward(queries, keys, values, tables, signed):
    pieces, rows, width = queries.shape
    whole = keys.shape[0]
    head, lanes, groups, count = attention_sizes(width)
    return pl.pallas_call(
        functools.partial(forward_kernel, head, count, signed),
        out_shape=(
            jax.ShapeDtypeStruct(queries.shape, BF),
            jax.ShapeDtypeStruct((pieces * groups, count, rows), F32),
        ),
        grid_spec=pltpu.PrefetchScalarGridSpec(
            num_scalar_prefetch=2,
            grid=(groups, pieces),
            in_specs=[
                pl.BlockSpec((1, rows, lanes), lambda g, i, b, o: (i, 0, g)),
                pl.BlockSpec((whole, rows, lanes), lambda g, i, b, o: (0, 0, g)),
                pl.BlockSpec((whole, rows, lanes), lambda g, i, b, o: (0, 0, g)),
            ],
            out_specs=[
                pl.BlockSpec((1, rows, lanes), lambda g, i, b, o: (i, 0, g)),
                pl.BlockSpec((1, count, rows), lambda g, i, b, o: (g * pieces + i, 0, 0)),
            ],
            scratch_shapes=[
                pltpu.VMEM((count, rows, min(128, lanes)), BF),
                pltpu.VMEM((whole, lanes, rows), BF),
                pltpu.VMEM((count, head, rows), F32),
                pltpu.VMEM((count, rows), F32),
            ],
        ),
        compiler_params=pltpu.CompilerParams(vmem_limit_bytes=20 * MIB),
        cost_estimate=pl.CostEstimate(flops=50_000_000_000, bytes_accessed=20_000_000, transcendentals=0),
    )(*tables, queries, keys, values)


def backward_kernel(
    head, count, signed, bounds, order, q_ref, do_ref, o_ref, lse_ref, k_ref, v_ref,
    dq_ref, dk_ref, dv_ref, qm, dom, kt, dq, dk, dv, delta,
):
    step = pl.program_id(1)
    whole, rows, lanes = k_ref.shape

    @pl.when(step == 0)
    def _():
        for j in range(whole):
            kt[j] = turned(k_ref[j]).astype(BF)
            dk[j] = jnp.zeros((rows, lanes), F32)
            dv[j] = jnp.zeros((rows, lanes), F32)

    for h, part in enumerate(head_parts(q_ref[0], head, count)):
        qm[h] = part
    for h, part in enumerate(head_parts(do_ref[0], head, count)):
        dom[h] = part
    product = jnp.transpose(do_ref[0].astype(F32) * o_ref[0].astype(F32))
    for h in range(count):
        delta[h : h + 1, :] = jnp.sum(product[h * head : (h + 1) * head], axis=0, keepdims=True)
    dq[...] = jnp.zeros_like(dq)
    start, last = bounds[step], bounds[OWN + step]

    def block(j, masked):
        keys, values = tiles_of(k_ref[j], head, count), tiles_of(v_ref[j], head, count)
        heads = range(count)
        scores = [dot(keys[h], qm[h], NT) for h in heads]
        dps = [dot(values[h], dom[h], NT) for h in heads]
        ps, dss = [], []
        for h, s, dp in zip(heads, scores, dps):
            if signed:
                square = s * s + 1.0
                inverse = lax.rsqrt(square)
                c = square * inverse
            else:
                c = s
            if masked:
                c = jnp.where(causal(c.shape), c, FLOOR)
            w = jnp.exp(c - lse_ref[0, h : h + 1, :])
            if signed:
                ratio = s * inverse
                slope = 1.0 + inverse * inverse * (inverse - 1.0)
                ps.append((w * ratio).astype(BF))
                dss.append((w * (dp * slope - delta[h : h + 1, :] * ratio)).astype(BF))
            else:
                ps.append(w.astype(BF))
                dss.append((w * (dp - delta[h : h + 1, :])).astype(BF))
        dvs, dks = [], []
        for h, p, ds in zip(heads, ps, dss):
            dvs.append(dot(p, dom[h]))
            dks.append(dot(ds, qm[h]))
            dq[h] += dot(kt[j, h * head : (h + 1) * head, :], ds)
        dv[j] += join_tiles(dvs, head)
        dk[j] += join_tiles(dks, head)

    @pl.loop(start, last)
    def _(j):
        block(order[j], False)

    block(step, True)
    turned_back = jnp.transpose(dq[...].reshape(count * head, rows)) * (head ** -0.5)
    dq_ref[0] = turned_back.astype(BF)

    @pl.when(step == pl.num_programs(1) - 1)
    def _():
        for j in range(whole):
            dk_ref[j] = dk[j].astype(BF)
            dv_ref[j] = dv[j].astype(BF)


def attend_backward(queries, grad_rows, attended, totals, keys, values, tables, signed, first, end):
    pieces, rows, width = queries.shape
    whole = keys.shape[0]
    head, lanes, groups, count = attention_sizes(width)
    own = pl.BlockSpec((1, rows, lanes), lambda g, i, b, o: (i, 0, g + first))
    every = pl.BlockSpec((whole, rows, lanes), lambda g, i, b, o: (0, 0, g + first))
    own_out = pl.BlockSpec((1, rows, lanes), lambda g, i, b, o: (i, 0, g))
    every_out = pl.BlockSpec((whole, rows, lanes), lambda g, i, b, o: (0, 0, g))
    spread = (end - first) * lanes
    return pl.pallas_call(
        functools.partial(backward_kernel, head, count, signed),
        out_shape=(
            jax.ShapeDtypeStruct((pieces, rows, spread), BF),
            jax.ShapeDtypeStruct((whole, rows, spread), BF),
            jax.ShapeDtypeStruct((whole, rows, spread), BF),
        ),
        grid_spec=pltpu.PrefetchScalarGridSpec(
            num_scalar_prefetch=2,
            grid=(end - first, pieces),
            in_specs=[
                own,
                own,
                own,
                pl.BlockSpec((1, count, rows), lambda g, i, b, o: ((g + first) * pieces + i, 0, 0)),
                every,
                every,
            ],
            out_specs=[own_out, every_out, every_out],
            scratch_shapes=[
                pltpu.VMEM((count, rows, min(128, lanes)), BF),
                pltpu.VMEM((count, rows, min(128, lanes)), BF),
                pltpu.VMEM((whole, lanes, rows), BF),
                pltpu.VMEM((count, head, rows), F32),
                pltpu.VMEM((whole, rows, lanes), F32),
                pltpu.VMEM((whole, rows, lanes), F32),
                pltpu.VMEM((count, rows), F32),
            ],
        ),
        compiler_params=pltpu.CompilerParams(vmem_limit_bytes=28 * MIB),
        cost_estimate=pl.CostEstimate(flops=25_000_000_000 * (end - first), bytes_accessed=10_000_000, transcendentals=0),
    )(*tables, queries, grad_rows, attended, totals, keys, values)


def xor_send(array, axis, bit):
    size = lax.axis_size(axis)
    return lax.ppermute(array, axis, [(i, i ^ bit) for i in range(size)])


def pick(array, index, axis=0):
    return lax.dynamic_index_in_dim(array, index, axis, keepdims=False)


def rows_at(array, index):
    return array.at[index].get(mode="promise_in_bounds")


def together(value, *others):
    return lax.optimization_barrier((value,) + others)[0]


def member_send(array, offset):
    if offset & 1:
        array = xor_send(array, "pb", 1)
    if offset >> 1:
        array = xor_send(array, "ka", offset >> 1)
    return array


def share_with_group(array, members):
    return jnp.concatenate([array] + [member_send(array, e) for e in range(1, members)], axis=0)


def plan_kernel(members, long, keys, me, held_piece, order, bounds, place, rank, by_rank, held):
    count = 4 * members

    def extremes(p, seen):
        return jnp.minimum(seen[0], keys[p]), jnp.maximum(seen[1], keys[p])

    least, most = lax.fori_loop(0, count, extremes, (keys[0], keys[0]))
    short = most - least >= long
    size = jnp.where(short, members // 2, members)

    def rank_one(p, _):
        r = lax.fori_loop(
            0, count, lambda q, r: r + jnp.where(keys[q] < keys[p], 1, 0), jnp.int32(0)
        )
        rank[p] = r
        by_rank[r] = p
        return 0

    lax.fori_loop(0, count, rank_one, 0)
    for e in range(members):
        member = me[0] ^ e
        second = jnp.where(short & (member >= members // 2), 1, 0)
        number = member - second * (members // 2)
        base = second * (2 * members)
        spread = (number, 2 * size - 1 - number, 2 * size + number, 4 * size - 1 - number)
        for i, r in enumerate(spread):
            held[4 * e + i] = base + r
            order[base + r] = 4 * e + i
            held_piece[4 * e + i] = by_rank[base + r]
            if e == 0:
                bounds[i] = base
                bounds[4 + i] = base + r

    def place_one(p, _):
        place[p] = order[rank[p]]
        return 0

    lax.fori_loop(0, count, place_one, 0)


def plan(keys, member, members, long):
    count = 4 * members
    smem = pl.BlockSpec(memory_space=pltpu.SMEM)
    table = jax.ShapeDtypeStruct((count,), jnp.int32)
    return pl.pallas_call(
        functools.partial(plan_kernel, members, long),
        out_shape=(table, table, jax.ShapeDtypeStruct((2 * OWN,), jnp.int32), table),
        in_specs=[smem, smem],
        out_specs=[smem] * 4,
        scratch_shapes=[pltpu.SMEM((count,), jnp.int32)] * 3,
    )(keys, jnp.reshape(member, (1,)).astype(jnp.int32))


class Layout:
    def __init__(self, sequence_ids, sequence_offsets):
        self.core = lax.axis_index("pb") % 2
        self.z = lax.axis_index("ka")
        self.depth = lax.axis_size("ka")
        self.subs = self.depth // 4
        self.members = self.depth // 2
        tall = sequence_ids.shape[0]
        self.rows = tall // OWN
        self.long = tall // BATCH * self.depth
        keys = (sequence_ids * self.long + sequence_offsets).reshape(OWN, self.rows)[:, :1]
        self.keys_under_way = self.send_in(
            jnp.broadcast_to(keys, (OWN, self.subs)).reshape(-1)
        )

    def settle(self):
        keys = self.arrived(self.keys_under_way).reshape(-1, self.subs)[:, 0]
        member = (self.z % self.subs) * 2 + self.core
        self.held_piece, self.order, self.bounds, self.place = plan(
            keys, member, self.members, self.long
        )
        self.tables = (self.bounds, self.order)

    def bits(self, place):
        return place // (2 * self.subs), place // self.subs % 2, place % self.subs

    def round_pairs(self, turn):
        pairs = []
        for pb in range(lax.axis_size("pb")):
            for z in range(self.depth):
                half, batch, sub = (a ^ b for a, b in zip(self.bits(z), self.bits(turn)))
                target = (2 * (pb % 2) + batch) * self.subs + sub
                pairs.append((pb * self.depth + z, (pb // 2 * 2 + half) * self.depth + target))
        return pairs

    def send_in(self, array):
        part_rows = array.shape[0] // (OWN * self.subs)
        blocks = array.reshape((BATCH, HALVES, self.subs, part_rows) + array.shape[1:])
        parts = []
        for turn in range(self.depth):
            half, batch, sub = (a ^ b for a, b in zip(self.bits(self.z), self.bits(turn)))
            part = pick(pick(pick(blocks, batch), half), sub)
            parts.append(lax.ppermute(part, ("pb", "ka"), self.round_pairs(turn)))
        return parts

    def arrived(self, parts):
        if self.subs == 1:
            return jnp.concatenate(parts + [xor_send(part, "pb", 1) for part in parts])
        held = jnp.concatenate(parts)
        part_rows, trailing = parts[0].shape[0], parts[0].shape[1:]
        held = held.reshape((4, self.subs, part_rows) + trailing)
        held = jnp.take(held, self.z % self.subs ^ jnp.arange(self.subs), axis=1)
        quarters = [[g * self.subs + i for i in range(self.subs)] for g in range(4)]
        held = lax.all_gather(held, "ka", axis=2, axis_index_groups=quarters)
        held = held.reshape((4 * self.subs * self.subs * part_rows,) + trailing)
        return jnp.concatenate([held, xor_send(held, "pb", 1)])


class Moving:
    def advance(self, value):
        self.launch(self.prepare(value))


class ScatterOut(Moving):
    def __init__(self, own, layout):
        self.layout = layout
        self.steps = ["first", "second", "assemble"]
        self.result = share_with_group(own, layout.members)

    def prepare(self, value):
        self.now = self.steps.pop(0) if self.steps else None
        turns = self.layout.depth // 2
        if self.now == "first":
            parts = self.parts(value)
            return parts[:turns], parts[turns:]
        return self.assemble(sum(value, [])) if self.now == "assemble" else value

    def launch(self, value):
        turns = self.layout.depth // 2
        if self.now == "first":
            value = (self.send(value[0], 0), value[1])
        elif self.now == "second":
            value = (value[0], self.send(value[1], turns))
        self.result = value

    def send(self, parts, first):
        return [
            lax.ppermute(part, ("pb", "ka"), [(b, a) for a, b in self.layout.round_pairs(turn)])
            for turn, part in enumerate(parts, first)
        ]

    def parts(self, shared):
        layout = self.layout
        subs = layout.subs
        rows, width = shared.shape[1:]
        shared = shared.reshape(-1, subs, rows // subs, width)
        sub = layout.z % subs
        parts = []
        for turn in range(layout.depth):
            piece = turn if subs == 1 else turn // subs * subs + (sub ^ turn % subs)
            parts.append(pick(pick(shared, pick(layout.place, piece)), sub))
        return parts

    def assemble(self, got):
        layout = self.layout
        subs = layout.subs
        order = []
        for block in range(OWN * subs):
            batch, half, part = block // (2 * subs), block // subs % 2, block % subs
            z_half, z_batch, z_sub = layout.bits(layout.z)
            order.append(((z_half ^ half) * 2 + (z_batch ^ batch)) * subs + (z_sub ^ part))
        return rows_at(jnp.stack(got), jnp.stack(order)).reshape(-1, got[0].shape[-1])


def stack_kernel(*refs):
    out, at = refs[-1], 0
    width = out.shape[1]
    for ref in refs[:-1]:
        for row in range(ref.shape[0]):
            for left in range(0, ref.shape[1], width):
                out[at : at + 1, :] = ref[row : row + 1, left : left + width]
                at += 1


def stack_rows(arrays):
    width = min(a.shape[1] for a in arrays)
    height = sum(a.size for a in arrays) // width
    vmem = pl.BlockSpec(memory_space=pltpu.VMEM)
    return pl.pallas_call(
        stack_kernel,
        out_shape=jax.ShapeDtypeStruct((height, width), F32),
        in_specs=[vmem] * len(arrays),
        out_specs=vmem,
        compiler_params=pltpu.CompilerParams(vmem_limit_bytes=4 * MIB),
    )(*arrays)


class VectorSum(Moving):
    def __init__(self, arrays):
        self.steps = []
        for axis in ("ka", "pb"):
            bits = lax.axis_size(axis).bit_length() - 1
            self.steps += [(axis, 1 << b) for b in range(bits)]
        self.result = stack_rows(arrays)

    def prepare(self, flat):
        self.now = self.steps.pop(0) if self.steps else None
        return flat

    def launch(self, flat):
        self.result = flat + xor_send(flat, *self.now) if self.now else flat


class BundleSum(Moving):
    def __init__(self, arrays, segments, at_once=False):
        self.along_pb, self.along_ka = lax.axis_size("pb"), lax.axis_size("ka")
        self.bits = self.along_pb.bit_length() - 1
        rest = list(range(1, self.bits))
        self.steps = ["core"] + list(zip(rest, rest[::-1]))
        self.steps += ["columns"] + list(range(1, self.along_ka.bit_length() - 1))
        self.narrow = arrays[0][0].shape[-1]
        self.segments = segments
        self.result = arrays
        if at_once:
            self.advance(arrays)

    def split(self, view, bit):
        axis = self.bits - 1 - bit
        own = (lax.axis_index("pb") >> bit) & 1
        kept = lax.dynamic_slice_in_dim(view, own, 1, axis)
        return kept, lax.dynamic_slice_in_dim(view, 1 - own, 1, axis)

    def prepare(self, views):
        self.now = step = self.steps.pop(0) if self.steps else None
        if step is None or step == "core":
            return views
        if isinstance(step, tuple):
            if len(views) == 1:
                half = views[0].shape[-2] // 2
                views = [views[0][..., :half, :], views[0][..., half:, :]]
            return [self.split(view, bit) for view, bit in zip(views, step)]
        if step == "columns":
            return split_columns(
                [v.reshape(-1, self.narrow) for v in views], self.segments, self.along_ka
            )
        own = (lax.axis_index("ka") >> step) & 1
        pairs = views.reshape((-1, 2) + views.shape[1:])
        return pick(pairs, own, 1), pick(pairs, 1 - own, 1)

    def launch(self, made):
        step = self.now
        if step is None:
            self.result = made
        elif step == "core":
            shape = (2,) * (self.bits - 1) + (1,)
            self.result = [
                (kept + xor_send(sent, "pb", 1)).reshape(shape + kept.shape[1:])
                for kept, sent in made
            ]
        elif isinstance(step, tuple):
            self.result = [
                kept + xor_send(sent, "pb", 1 << bit) for (kept, sent), bit in zip(made, step)
            ]
        else:
            kept, sent = made
            got = xor_send(sent, "ka", 1 if step == "columns" else 1 << step)
            self.result = kept + got if self.steps else [kept[0], got[0]]

    def matrices(self):
        return join_columns(self.result, self.segments, self.narrow, self.along_ka)


def split_kernel(segments, ways, z, *refs):
    views, (kept, sent, whole) = refs[:-3], refs[-3:]
    at = 0
    for view in views:
        whole[at : at + view.shape[0], :] = view[...]
        at += view.shape[0]
    narrow = whole.shape[1]
    thin = narrow // ways
    for target in range(ways):
        pieces, at = [], 0
        for height, folds in segments:
            share = ways // folds
            first = at + target // share * height
            wide = narrow // share
            for i in range(wide // thin):
                left = target % share * wide + i * thin
                pieces.append(whole[first : first + height, left : left + thin])
            at += height * folds
        rows = jnp.concatenate(pieces, axis=0)
        half = rows.shape[0] // 2
        block = jnp.concatenate([rows[:half], rows[half:]], axis=1)
        mine = z[0] % 2 == target % 2

        @pl.when(mine)
        def _():
            kept[target // 2] = block

        @pl.when(jnp.logical_not(mine))
        def _():
            sent[target // 2] = block


def split_columns(views, segments, ways):
    narrow = views[0].shape[1]
    height = sum(v.shape[0] for v in views)
    shape = jax.ShapeDtypeStruct((ways // 2, height // 2, 2 * narrow // ways), BF)
    vmem = pl.BlockSpec(memory_space=pltpu.VMEM)
    return pl.pallas_call(
        functools.partial(split_kernel, segments, ways),
        out_shape=[shape] * 2,
        in_specs=[pl.BlockSpec(memory_space=pltpu.SMEM)] + [vmem] * len(views),
        out_specs=[vmem] * 2,
        scratch_shapes=[pltpu.VMEM((height, narrow), BF)],
        compiler_params=pltpu.CompilerParams(vmem_limit_bytes=16 * MIB),
    )(lax.axis_index("ka").reshape(1).astype(jnp.int32), *views)


def join_kernel(segments, narrow, ways, *refs):
    outs = refs[2:]
    total = refs[0][...].astype(F32) + refs[1][...].astype(F32)
    thin = narrow // ways
    rows = jnp.concatenate([total[:, :thin], total[:, thin:]], axis=0)
    at = 0
    for (height, folds), out in zip(segments, outs):
        pieces = [rows[at + i * height : at + (i + 1) * height] for i in range(folds)]
        out[...] = pieces[0] if folds == 1 else jnp.concatenate(pieces, axis=1)
        at += height * folds


def join_columns(parts, segments, narrow, ways):
    vmem = pl.BlockSpec(memory_space=pltpu.VMEM)
    thin = narrow // ways
    return pl.pallas_call(
        functools.partial(join_kernel, segments, narrow, ways),
        out_shape=[jax.ShapeDtypeStruct((height, thin * folds), F32) for height, folds in segments],
        in_specs=[vmem] * 2,
        out_specs=[vmem] * len(segments),
        compiler_params=pltpu.CompilerParams(vmem_limit_bytes=16 * MIB),
    )(*parts)


class Background:
    def __init__(self):
        self.moving = []

    def tick(self, value):
        live = [m for m in self.moving if not getattr(m, "ended", False)]
        value, results = lax.optimization_barrier((value, [m.result for m in live]))
        for m in live:
            m.ended = not m.steps
        made = [m.prepare(r) for m, r in zip(live, results)]
        value, made = lax.optimization_barrier((value, made))
        for m, parts in zip(live, made):
            m.launch(parts)
        return value

    def drain(self):
        for m in self.moving:
            while m.steps:
                m.advance(m.result)


def normalized(values):
    centre = values - jnp.mean(values, axis=-1, keepdims=True)
    spread = jnp.mean(centre * centre, axis=-1, keepdims=True)
    scale = lax.rsqrt(spread + EPSILON)
    return centre * scale, scale


def layer_norm(values, gain, shift):
    return (normalized(values)[0] * gain.astype(F32) + shift.astype(F32)).astype(BF)


def norm_backward(values, gain, upstream):
    n, scale = normalized(values)
    vectors = jnp.sum(jnp.stack([upstream * n, upstream]), axis=1)
    dn = upstream * gain.astype(F32)
    mean = jnp.mean(dn, axis=-1, keepdims=True)
    along = jnp.mean(dn * n, axis=-1, keepdims=True)
    return scale * (dn - mean - n * along), vectors


def gelu_pair(u):
    size = jnp.abs(u) * 0.7071067811865476
    t = 1.0 / (1.0 + 0.3275911 * size)
    bell = jnp.exp(-0.5 * u * u)
    series = t * (
        0.254829592
        + t * (-0.284496736 + t * (1.421413741 + t * (-1.453152027 + t * 1.061405429)))
    )
    tail = 0.5 * series * bell
    phi = jnp.where(u < 0, tail, 1.0 - tail)
    return u * phi, phi + u * (bell * 0.3989422804014327)


def row_tiles(tall):
    tile = min(256, tall)
    return [slice(r, r + tile) for r in range(0, tall, tile)]


def norm_rows(values, gain, shift):
    centre = values - jnp.mean(values, axis=-1, keepdims=True)
    spread = jnp.mean(centre * centre, axis=-1, keepdims=True)
    return (centre * lax.rsqrt(spread + EPSILON) * gain + shift).astype(BF)


def mlp_kernel(
    following, o_ref, x_ref, wo_ref, gain_ref, bias_ref, wu_ref, ub_ref, wd_ref, db_ref, ng_ref, nb_ref,
    x1_ref, h2_ref, a_ref, s_ref, y_ref, *rest,
):
    acc = rest[-1]
    step = pl.program_id(0)
    tiles = row_tiles(o_ref.shape[0])

    @pl.when(step == 0)
    def _():
        gain, shift = gain_ref[...].astype(F32), bias_ref[...].astype(F32)
        for t in tiles:
            x1 = x_ref[t].astype(F32) + dot(o_ref[t], wo_ref[...])
            x1_ref[t] = x1
            h2_ref[t] = norm_rows(x1, gain, shift)
            acc[t] = jnp.zeros_like(x1)

    up_bias = ub_ref[...].astype(F32)
    hidden = [dot(h2_ref[t], wu_ref[...]) for t in tiles]
    actives = []
    for t, u in zip(tiles, hidden):
        active, slope = gelu_pair(u + up_bias)
        actives.append(active.astype(BF))
        a_ref[t] = actives[-1]
        s_ref[t] = slope.astype(BF)
    for t, active in zip(tiles, actives):
        acc[t] += dot(active, wd_ref[...])

    @pl.when(step == pl.num_programs(0) - 1)
    def _():
        down_bias = db_ref[...].astype(F32)
        gain, shift = ng_ref[...].astype(F32), nb_ref[...].astype(F32)
        for t in tiles:
            y = x1_ref[t] + (acc[t] + down_bias)
            y_ref[t] = y.astype(y_ref.dtype)
            if following:
                rest[0][t] = norm_rows(y, gain, shift)


ONCE = pl.Buffered(1)


def whole_block(array):
    return pl.BlockSpec(array.shape, lambda i: (0,) * len(array.shape), pipeline_mode=ONCE)


def cost(flops, *arrays):
    moved = sum(a.size * a.dtype.itemsize for a in arrays)
    return pl.CostEstimate(flops=flops, bytes_accessed=moved, transcendentals=0)


def mlp_forward(attended, x_own, params, following):
    (_, _, _, _, _, w_out, mlp_gain, mlp_bias, w_up, up_bias, w_down, down_bias) = params
    tall, width = attended.shape
    hidden = w_up.shape[1]
    row = lambda v: v.reshape(1, -1)
    gain, shift = following or (mlp_gain, mlp_bias)
    inputs = (
        attended, x_own, w_out, row(mlp_gain), row(mlp_bias), w_up, row(up_bias), w_down,
        row(down_bias), row(gain), row(shift),
    )
    specs = [whole_block(a) for a in inputs]
    specs[5] = pl.BlockSpec((width, width), lambda i: (0, i))
    specs[6] = pl.BlockSpec((1, width), lambda i: (0, i))
    specs[7] = pl.BlockSpec((width, width), lambda i: (i, 0))
    wide, narrow = (tall, hidden), (tall, width)
    shapes = [(narrow, F32), (narrow, BF), (wide, BF), (wide, BF), (narrow, F32 if following else BF)]
    shapes += [(narrow, BF)] if following else []
    out_shape = [jax.ShapeDtypeStruct(shape, kind) for shape, kind in shapes]
    chunk = pl.BlockSpec((tall, width), lambda i: (0, i))
    full = pl.BlockSpec((tall, width), lambda i: (0, 0), pipeline_mode=ONCE)
    return pl.pallas_call(
        functools.partial(mlp_kernel, following is not None),
        out_shape=out_shape,
        grid=(hidden // width,),
        in_specs=specs,
        out_specs=[full, full, chunk, chunk, full] + ([full] if following else []),
        scratch_shapes=[pltpu.VMEM((tall, width), F32)],
        compiler_params=pltpu.CompilerParams(vmem_limit_bytes=36 * MIB),
        cost_estimate=cost(2 * tall * width * (2 * hidden + width), *inputs, *out_shape),
    )(*inputs)


def mlp_back_kernel(
    g_ref, slope_ref, wd_ref, wu_ref, x1_ref, gain_ref, wo_ref,
    du_ref, dx_ref, gx_ref, do_ref, gb_ref, sums_ref, vectors_ref, acc,
):
    step = pl.program_id(0)
    tiles = row_tiles(g_ref.shape[0])

    @pl.when(step == 0)
    def _():
        for t in tiles:
            gb_ref[t] = g_ref[t].astype(BF)
            acc[t] = jnp.zeros(acc[t].shape, F32)

    total = 0.0
    products = [dot(gb_ref[t], wd_ref[...], NT) for t in tiles]
    for t, da in zip(tiles, products):
        du = (da * slope_ref[t].astype(F32)).astype(BF)
        du_ref[t] = du
        total = total + jnp.sum(du.astype(F32), axis=0, keepdims=True)
        acc[t] += dot(du, wu_ref[...], NT)
    sums_ref[...] = total

    @pl.when(step == pl.num_programs(0) - 1)
    def _():
        gain = gain_ref[...].astype(F32)
        of_gain = of_shift = of_down = 0.0
        for t in tiles:
            dh2, x1 = acc[t], x1_ref[t]
            centre = x1 - jnp.mean(x1, axis=-1, keepdims=True)
            scale = lax.rsqrt(jnp.mean(centre * centre, axis=-1, keepdims=True) + EPSILON)
            n = centre * scale
            of_gain = of_gain + jnp.sum(dh2 * n, axis=0, keepdims=True)
            of_shift = of_shift + jnp.sum(dh2, axis=0, keepdims=True)
            of_down = of_down + jnp.sum(gb_ref[t].astype(F32), axis=0, keepdims=True)
            dn = dh2 * gain
            mean = jnp.mean(dn, axis=-1, keepdims=True)
            along = jnp.mean(dn * n, axis=-1, keepdims=True)
            dx = g_ref[t].astype(F32) + scale * (dn - mean - n * along)
            dx_ref[t] = dx
            gx = dx.astype(BF)
            gx_ref[t] = gx
            do_ref[t] = dot(gx, wo_ref[...], NT).astype(BF)
        vectors_ref[0:1, :] = of_gain
        vectors_ref[1:2, :] = of_shift
        vectors_ref[2:3, :] = of_down


def mlp_backward(upstream, slope, middle, params):
    (_, _, _, _, _, w_out, mlp_gain, _, w_up, _, w_down, _) = params
    tall, width = upstream.shape
    hidden = slope.shape[1]
    inputs = (upstream, slope, w_down, w_up, middle, mlp_gain.reshape(1, -1), w_out)
    specs = [whole_block(a) for a in inputs]
    specs[1] = pl.BlockSpec((tall, width), lambda i: (0, i))
    specs[2] = pl.BlockSpec((width, width), lambda i: (i, 0))
    specs[3] = pl.BlockSpec((width, width), lambda i: (0, i))
    shapes = [((tall, hidden), BF), ((tall, width), F32)] + [((tall, width), BF)] * 3
    shapes += [((1, hidden), F32), ((3, width), F32)]
    out_shape = [jax.ShapeDtypeStruct(shape, kind) for shape, kind in shapes]
    full = pl.BlockSpec((tall, width), lambda i: (0, 0), pipeline_mode=ONCE)
    return pl.pallas_call(
        mlp_back_kernel,
        out_shape=out_shape,
        grid=(hidden // width,),
        in_specs=specs,
        out_specs=[
            pl.BlockSpec((tall, width), lambda i: (0, i)), full, full, full, full,
            pl.BlockSpec((1, width), lambda i: (0, i)), pl.BlockSpec((3, width), lambda i: (0, 0)),
        ],
        scratch_shapes=[pltpu.VMEM((tall, width), F32)],
        compiler_params=pltpu.CompilerParams(vmem_limit_bytes=40 * MIB),
        cost_estimate=cost(2 * tall * width * (2 * hidden + width), *inputs, *out_shape),
    )(*inputs)


def put_halves(core, kept_ref, sent_ref, low, high):
    @pl.when(core == 0)
    def _():
        kept_ref[...] = low
        sent_ref[...] = high

    @pl.when(core != 0)
    def _():
        kept_ref[...] = high
        sent_ref[...] = low


def by_blocks(product, blocks):
    height, breadth = product.shape
    parts = product.astype(BF).reshape(blocks // 2, 2, height // blocks, breadth)
    return parts[:, 0], parts[:, 1]


def mlp_weights_kernel(
    blocks, folds, core, h2_ref, du_ref, o_ref, gx_ref, a_ref, gb_ref,
    kept_a, sent_a, kept_b, sent_b,
):
    step = pl.program_id(0)

    @pl.when(step < folds)
    def _():
        put_halves(core[0], kept_a, sent_a, *by_blocks(dot(h2_ref[...], du_ref[...], TN), blocks))

    @pl.when(step == folds)
    def _():
        put_halves(core[0], kept_a, sent_a, *by_blocks(dot(o_ref[...], gx_ref[...], TN), blocks))

    @pl.when(step > folds)
    def _():
        product = dot(a_ref[...], gb_ref[...], TN)
        pairs, _, height, _ = kept_b.shape
        parts = product.astype(BF).reshape(pairs, 1, 2, height, product.shape[1])
        put_halves(core[0], kept_b, sent_b, parts[:, :, 0], parts[:, :, 1])


def mlp_weights(h2, du, attended, gx, active, gb):
    blocks = lax.axis_size("pb")
    tall, width = h2.shape
    hidden = du.shape[1]
    folds = hidden // width
    thin, tall_block = width // blocks, hidden // blocks
    pairs = blocks // 2 // folds
    full = pl.BlockSpec((tall, width), lambda i, c: (0, 0), pipeline_mode=ONCE)
    a_block = pl.BlockSpec(
        (blocks // 2, thin, width), lambda i, c: (0, jnp.minimum(i, folds), 0)
    )
    b_block = pl.BlockSpec(
        (pairs, 1, tall_block, width), lambda i, c: (jnp.maximum(i - folds - 1, 0), 0, 0, 0)
    )
    a_shape = jax.ShapeDtypeStruct((blocks // 2, thin * (folds + 1), width), BF)
    b_shape = jax.ShapeDtypeStruct((blocks // 2, 1, tall_block, width), BF)
    core = (lax.axis_index("pb") % 2).reshape(1).astype(jnp.int32)
    inputs = (h2, du, attended, gx, active, gb)
    kept_a, sent_a, kept_b, sent_b = pl.pallas_call(
        functools.partial(mlp_weights_kernel, blocks, folds),
        out_shape=(a_shape, a_shape, b_shape, b_shape),
        grid_spec=pltpu.PrefetchScalarGridSpec(
            num_scalar_prefetch=1,
            grid=(2 * folds + 1,),
            in_specs=[
                full,
                pl.BlockSpec((tall, width), lambda i, c: (0, jnp.minimum(i, folds - 1))),
                full,
                full,
                pl.BlockSpec((tall, width), lambda i, c: (0, jnp.clip(i - folds - 1, 0, folds - 1))),
                full,
            ],
            out_specs=[a_block, a_block, b_block, b_block],
        ),
        compiler_params=pltpu.CompilerParams(vmem_limit_bytes=32 * MIB),
        cost_estimate=cost(2 * tall * width * (2 * hidden + width), *inputs, a_shape, b_shape),
    )(core, *inputs)
    flat = lambda v: v.reshape(blocks // 2, tall_block, width)
    arrays = [(kept_a, sent_a), (flat(kept_b), flat(sent_b))]
    return BundleSum(arrays, [(thin, folds), (thin, 1), (tall_block, 1)])


def attention_weights_kernel(blocks, core, *refs):
    h_ref, kept_ref, sent_ref = refs[0], refs[-2], refs[-1]
    parts = refs[1:-2]
    count = len(parts) // 3
    for which in range(3):

        @pl.when(pl.program_id(0) == which)
        def _():
            products = [
                dot(h_ref[: part.shape[0], :], part[...], TN)
                for part in parts[which * count : (which + 1) * count]
            ]
            product = products[0] if count == 1 else jnp.concatenate(products, axis=1)
            put_halves(core[0], kept_ref, sent_ref, *by_blocks(product, blocks))


def attention_weights(h_all, dqs, dks, dvs):
    blocks = lax.axis_size("pb")
    width = h_all.shape[1]
    thin = width // blocks
    inputs = (h_all, *dqs, *dks, *dvs)
    block = pl.BlockSpec((blocks // 2, thin, width), lambda i, c: (0, i, 0))
    shape = jax.ShapeDtypeStruct((blocks // 2, 3 * thin, width), BF)
    core = (lax.axis_index("pb") % 2).reshape(1).astype(jnp.int32)
    kept, sent = pl.pallas_call(
        functools.partial(attention_weights_kernel, blocks),
        out_shape=(shape, shape),
        grid_spec=pltpu.PrefetchScalarGridSpec(
            num_scalar_prefetch=1,
            grid=(3,),
            in_specs=[
                pl.BlockSpec(a.shape, lambda i, c: (0, 0), pipeline_mode=ONCE) for a in inputs
            ],
            out_specs=[block, block],
        ),
        compiler_params=pltpu.CompilerParams(vmem_limit_bytes=28 * MIB),
        cost_estimate=cost(5 * h_all.shape[0] * width * width, *inputs, shape),
    )(core, *inputs)
    return BundleSum([(kept, sent)], [(thin, 1)] * 3, at_once=True)


def layer_forward(x_own, h_all, params, layout, signed, passing, following):
    (_, _, w_query, w_key, w_value, *_) = params
    tall, width = x_own.shape
    rows = layout.rows
    scale = (width // HEADS) ** -0.5
    queries = (dense(h_all[:tall], w_query, 1, 0) * scale).astype(BF).reshape(OWN, rows, width)
    keys = dense(h_all, w_key, 1, 0).astype(BF).reshape(-1, rows, width)
    values = dense(h_all, w_value, 1, 0).astype(BF).reshape(-1, rows, width)
    attended, totals = attend_forward(queries, keys, values, layout.tables, signed)
    (attended, totals), passing = lax.optimization_barrier(((attended, totals), passing))
    middle, h2, active, slope, *result = mlp_forward(
        attended.reshape(tall, width), x_own, params, following
    )
    saved = (h_all, queries, keys, values, attended, totals, middle, h2, active, slope)
    return result, saved, passing


def layer_backward(upstream, x_own, params, saved, layout, signed, background, cuts, earlier):
    (norm_gain, _, w_query, w_key, w_value, *_) = params
    h_all, queries, keys, values, attended, totals, middle, h2, active, slope = saved
    tall, width = x_own.shape
    du, dx1, gx, do, gb, sum_du, vectors = mlp_backward(upstream, slope, middle, params)
    mlp_vectors = [vectors, sum_du]
    if earlier:
        du, gx, do, gb = background.tick((du, gx, do, gb))
    sum_mlp = mlp_weights(h2, du, attended.reshape(tall, width), gx, active, gb)
    background.moving.append(sum_mlp)
    sum_vectors = VectorSum(earlier + mlp_vectors) if earlier else None
    if earlier:
        background.moving.append(sum_vectors)
    do = do.reshape(queries.shape)
    outcome = []
    for first, end in zip(cuts, cuts[1:]):
        do = background.tick(do)
        if end > first:
            outcome.append(
                attend_backward(
                    queries, do, attended, totals, keys, values, layout.tables, signed, first, end
                )
            )
            do = together(do, outcome[-1])
    outcome = background.tick(outcome)
    dqs, dks, dvs = ([p.reshape(-1, p.shape[-1]) for p in parts] for parts in zip(*outcome))
    dq, dk, dv = (jnp.concatenate(parts, axis=-1) for parts in (dqs, dks, dvs))
    from_keys = (dense(dk, w_key, 1, 1) + dense(dv, w_value, 1, 1)).astype(BF)
    (dqs, dks, dvs), from_keys = lax.optimization_barrier(((dqs, dks, dvs), from_keys))
    from_keys = from_keys.reshape(layout.members, tall, width)
    given = [member_send(from_keys[e], e) for e in range(1, layout.members)]
    dh = dense(dq, w_query, 1, 1) + from_keys[0].astype(F32)
    sum_att = attention_weights(h_all, dqs, dks, dvs)
    background.moving.append(sum_att)
    for part in given:
        dh = dh + part.astype(F32)
    dx, norm_vectors = norm_backward(x_own.astype(F32), norm_gain, dh)

    def finish(mlp, norm):
        up, out, down = sum_mlp.matrices()
        query, key, value = sum_att.matrices()
        return (
            norm[0], norm[1], query, key, value, out,
            mlp[0], mlp[1], up, mlp[3:].reshape(-1), down, mlp[2],
        )

    return dx1 + dx, mlp_vectors, norm_vectors, sum_vectors, finish


def per_device(tokens, sequence_ids, sequence_offsets, *rest):
    signed_params, plain_params, cotangent = rest[:12], rest[12:24], rest[24]
    tall, width = tokens.shape
    layout = Layout(sequence_ids, sequence_offsets)
    tokens, layout.keys_under_way = lax.optimization_barrier((tokens, layout.keys_under_way))
    rows = layout.rows
    background = Background()
    x_all = layout.arrived(layout.send_in(tokens)).reshape(-1, rows, width)
    layout.settle()
    x_held = rows_at(x_all, layout.held_piece).reshape(-1, width)
    cotangent = layout.send_in(together(cotangent, x_held))
    h_all = layer_norm(x_held.astype(F32), signed_params[0], signed_params[1])
    x_own = x_held[:tall]
    (between, h_own), signed_saved, cotangent = layer_forward(
        x_own, h_all, signed_params, layout, True, cotangent, plain_params[:2]
    )
    h_all = share_with_group(h_own, layout.members)
    upstream = layout.arrived(cotangent).reshape(-1, rows, width)
    (final,), plain_saved, upstream = layer_forward(
        between, h_all, plain_params, layout, False, upstream, None
    )
    output = ScatterOut(final.reshape(OWN, rows, width), layout)
    background.moving.append(output)
    upstream = rows_at(upstream, layout.held_piece[:OWN]).reshape(tall, width)
    groups = attention_sizes(width)[2]
    upstream, mlp_plain, norm_plain, _, finish_plain = layer_backward(
        upstream, between, plain_params, plain_saved, layout, False, background,
        (0, groups // 3, groups), [],
    )
    upstream = background.tick(upstream)
    upstream, _, norm_signed, early, finish_signed = layer_backward(
        upstream, x_own, signed_params, signed_saved, layout, True, background,
        tuple(range(groups + 1)), mlp_plain + [norm_plain],
    )
    upstream = background.tick(upstream)
    back = ScatterOut(upstream.astype(BF).reshape(OWN, rows, width), layout)
    late = VectorSum([norm_signed])
    for _ in range(2):
        late.advance(late.result)
    background.moving += [back, late]
    background.tick(())
    background.tick(())
    background.drain()
    count = signed_params[8].shape[1] // width + 3
    early, late = early.result, late.result
    return (
        (output.result, back.result.astype(F32))
        + finish_signed(early[count + 2 :], late)
        + finish_plain(early[:count], early[count : count + 2])
    )


def solution(mesh):
    rows, block = P(("pb", "ka"), None), P("pb", "ka")
    grads = (P(), P(), block, block, block, block, P(), P(), block, P(), block, P())
    return jax.shard_map(
        per_device,
        mesh=mesh,
        in_specs=(rows, P(("pb", "ka")), P(("pb", "ka"))) + (P(),) * 24 + (rows,),
        out_specs=(rows, rows) + grads + grads,
        check_vma=False,
    )
```

```python
import functools

import jax
import jax.numpy as jnp
from jax import lax
from jax.experimental import pallas as pl
from jax.experimental.pallas import tpu as pltpu
from jax.sharding import PartitionSpec as P

HEADS = 12
BATCH = 2
HALVES = 2
OWN = BATCH * HALVES
EPSILON = 1e-05
FLOOR = -1e30
LEAST, MOST = 1e-25, 1e30
BF = jnp.bfloat16
F32 = jnp.float32
MIB = 1 << 20

NT = (((1,), (1,)), ((), ()))
NN = (((1,), (0,)), ((), ()))
TN = (((0,), (0,)), ((), ()))


def dot(left, right, dims=NN):
    return lax.dot_general(left, right, dims, preferred_element_type=F32)


def dense(left, right, left_axis, right_axis):
    return lax.dot_general(
        left, right, (((left_axis,), (right_axis,)), ((), ())), preferred_element_type=F32
    )


def attention_sizes(width):
    head = width // HEADS
    lanes = 256
    while width % lanes or lanes % head:
        lanes //= 2
    return head, lanes, width // lanes, lanes // head


def head_parts(block, head, count):
    tile = min(128, block.shape[1])
    per = tile // head
    lane = lax.broadcasted_iota(jnp.int32, (block.shape[0], tile), 1) // head
    tiles = [block[:, t : t + tile] for t in range(0, block.shape[1], tile)]
    zero = jnp.zeros_like(tiles[0])
    return [jnp.where(lane == h % per, tiles[h // per], zero) for h in range(count)]


def tiles_of(block, head, count):
    tile = min(128, block.shape[1])
    per = tile // head
    tiles = [block[:, t : t + tile] for t in range(0, block.shape[1], tile)]
    return [tiles[h // per] for h in range(count)]


def join_tiles(parts, head):
    per = parts[0].shape[1] // head
    sums = [sum(parts[h + 1 : h + per], parts[h]) for h in range(0, len(parts), per)]
    return sums[0] if len(sums) == 1 else jnp.concatenate(sums, axis=1)


def turned(block):
    return jnp.transpose(block.astype(F32))


def causal(shape):
    key = lax.broadcasted_iota(jnp.int32, shape, 0)
    query = lax.broadcasted_iota(jnp.int32, shape, 1)
    return key <= query


def forward_kernel(head, count, signed, bounds, order, q_ref, k_ref, v_ref, o_ref, lse_ref, qm, vt, acc, sums):
    step = pl.program_id(1)

    @pl.when(step == 0)
    def _():
        for j in range(k_ref.shape[0]):
            vt[j] = turned(v_ref[j]).astype(BF)

    for h, part in enumerate(head_parts(q_ref[0], head, count)):
        qm[h] = part
    rows = q_ref.shape[1]
    start, last = bounds[step], bounds[OWN + step]

    def scores(j):
        return [dot(keys, qm[h], NT) for h, keys in enumerate(tiles_of(k_ref[j], head, count))]

    def magnitude(s, masked):
        c, ratio = s, None
        if signed:
            square = s * s + 1.0
            inverse = lax.rsqrt(square)
            c, ratio = square * inverse, s * inverse
        if masked:
            c = jnp.where(causal(c.shape), c, FLOOR)
        return c, ratio

    def weigh(j, h, raised, ratio):
        if signed:
            raised = raised * ratio
        return dot(vt[j, h * head : (h + 1) * head, :], raised.astype(BF))

    def plain_block(j, carry, masked):
        result = []
        for h, s in enumerate(scores(j)):
            c, ratio = magnitude(s, masked)
            raised = jnp.exp(c)
            result.append(carry[h] + jnp.sum(raised, axis=0, keepdims=True))
            acc[h] += weigh(j, h, raised, ratio)
        return tuple(result)

    def safe_block(j, carry, masked):
        result = []
        for h, s in enumerate(scores(j)):
            top, total = carry[2 * h], carry[2 * h + 1]
            c, ratio = magnitude(s, masked)
            higher = jnp.maximum(top, jnp.max(c, axis=0, keepdims=True))
            raised = jnp.exp(c - higher)
            fade = jnp.exp(top - higher)
            acc[h] = acc[h] * fade + weigh(j, h, raised, ratio)
            result += [higher, total * fade + jnp.sum(raised, axis=0, keepdims=True)]
        return tuple(result)

    def over_keys(block, first):
        acc[...] = jnp.zeros_like(acc)
        carry = lax.fori_loop(start, last, lambda j, c: block(order[j], c, False), first)
        return block(step, carry, True)

    zeros = jnp.zeros((1, rows), F32)
    totals = jnp.concatenate(over_keys(plain_block, (zeros,) * count), axis=0)
    fine = jnp.min(jnp.where((totals > LEAST) & (totals < MOST), 1.0, 0.0)) > 0.5
    sums[...] = totals
    lse_ref[0] = jnp.log(totals)

    @pl.when(jnp.logical_not(fine))
    def _():
        carry = over_keys(safe_block, (zeros + FLOOR, zeros) * count)
        for h in range(count):
            sums[h : h + 1, :] = carry[2 * h + 1]
            lse_ref[0, h : h + 1, :] = carry[2 * h] + jnp.log(carry[2 * h + 1])

    share = 1.0 / sums[...]
    for h in range(count):
        acc[h] = acc[h] * share[h : h + 1, :]
    o_ref[0] = jnp.transpose(acc[...].reshape(count * head, rows)).astype(BF)


def attend_forward(queries, keys, values, tables, signed):
    pieces, rows, width = queries.shape
    whole = keys.shape[0]
    head, lanes, groups, count = attention_sizes(width)
    return pl.pallas_call(
        functools.partial(forward_kernel, head, count, signed),
        out_shape=(
            jax.ShapeDtypeStruct(queries.shape, BF),
            jax.ShapeDtypeStruct((pieces * groups, count, rows), F32),
        ),
        grid_spec=pltpu.PrefetchScalarGridSpec(
            num_scalar_prefetch=2,
            grid=(groups, pieces),
            in_specs=[
                pl.BlockSpec((1, rows, lanes), lambda g, i, b, o: (i, 0, g)),
                pl.BlockSpec((whole, rows, lanes), lambda g, i, b, o: (0, 0, g)),
                pl.BlockSpec((whole, rows, lanes), lambda g, i, b, o: (0, 0, g)),
            ],
            out_specs=[
                pl.BlockSpec((1, rows, lanes), lambda g, i, b, o: (i, 0, g)),
                pl.BlockSpec((1, count, rows), lambda g, i, b, o: (g * pieces + i, 0, 0)),
            ],
            scratch_shapes=[
                pltpu.VMEM((count, rows, min(128, lanes)), BF),
                pltpu.VMEM((whole, lanes, rows), BF),
                pltpu.VMEM((count, head, rows), F32),
                pltpu.VMEM((count, rows), F32),
            ],
        ),
        compiler_params=pltpu.CompilerParams(vmem_limit_bytes=20 * MIB),
        cost_estimate=pl.CostEstimate(flops=50_000_000_000, bytes_accessed=20_000_000, transcendentals=0),
    )(*tables, queries, keys, values)


def backward_kernel(
    head, count, signed, bounds, order, q_ref, do_ref, o_ref, lse_ref, k_ref, v_ref,
    dq_ref, dk_ref, dv_ref, qm, dom, kt, dq, dk, dv, delta,
):
    step = pl.program_id(1)
    whole, rows, lanes = k_ref.shape

    @pl.when(step == 0)
    def _():
        for j in range(whole):
            kt[j] = turned(k_ref[j]).astype(BF)
            dk[j] = jnp.zeros((rows, lanes), F32)
            dv[j] = jnp.zeros((rows, lanes), F32)

    for h, part in enumerate(head_parts(q_ref[0], head, count)):
        qm[h] = part
    for h, part in enumerate(head_parts(do_ref[0], head, count)):
        dom[h] = part
    product = jnp.transpose(do_ref[0].astype(F32) * o_ref[0].astype(F32))
    for h in range(count):
        delta[h : h + 1, :] = jnp.sum(product[h * head : (h + 1) * head], axis=0, keepdims=True)
    dq[...] = jnp.zeros_like(dq)
    start, last = bounds[step], bounds[OWN + step]

    def block(j, masked):
        keys, values = tiles_of(k_ref[j], head, count), tiles_of(v_ref[j], head, count)
        heads = range(count)
        scores = [dot(keys[h], qm[h], NT) for h in heads]
        dps = [dot(values[h], dom[h], NT) for h in heads]
        ps, dss = [], []
        for h, s, dp in zip(heads, scores, dps):
            if signed:
                square = s * s + 1.0
                inverse = lax.rsqrt(square)
                c = square * inverse
            else:
                c = s
            if masked:
                c = jnp.where(causal(c.shape), c, FLOOR)
            w = jnp.exp(c - lse_ref[0, h : h + 1, :])
            if signed:
                ratio = s * inverse
                slope = 1.0 + inverse * inverse * (inverse - 1.0)
                ps.append((w * ratio).astype(BF))
                dss.append((w * (dp * slope - delta[h : h + 1, :] * ratio)).astype(BF))
            else:
                ps.append(w.astype(BF))
                dss.append((w * (dp - delta[h : h + 1, :])).astype(BF))
        dvs, dks = [], []
        for h, p, ds in zip(heads, ps, dss):
            dvs.append(dot(p, dom[h]))
            dks.append(dot(ds, qm[h]))
            dq[h] += dot(kt[j, h * head : (h + 1) * head, :], ds)
        dv[j] += join_tiles(dvs, head)
        dk[j] += join_tiles(dks, head)

    @pl.loop(start, last)
    def _(j):
        block(order[j], False)

    block(step, True)
    turned_back = jnp.transpose(dq[...].reshape(count * head, rows)) * (head ** -0.5)
    dq_ref[0] = turned_back.astype(BF)

    @pl.when(step == pl.num_programs(1) - 1)
    def _():
        for j in range(whole):
            dk_ref[j] = dk[j].astype(BF)
            dv_ref[j] = dv[j].astype(BF)


def attend_backward(queries, grad_rows, attended, totals, keys, values, tables, signed, first, end):
    pieces, rows, width = queries.shape
    whole = keys.shape[0]
    head, lanes, groups, count = attention_sizes(width)
    own = pl.BlockSpec((1, rows, lanes), lambda g, i, b, o: (i, 0, g + first))
    every = pl.BlockSpec((whole, rows, lanes), lambda g, i, b, o: (0, 0, g + first))
    own_out = pl.BlockSpec((1, rows, lanes), lambda g, i, b, o: (i, 0, g))
    every_out = pl.BlockSpec((whole, rows, lanes), lambda g, i, b, o: (0, 0, g))
    spread = (end - first) * lanes
    return pl.pallas_call(
        functools.partial(backward_kernel, head, count, signed),
        out_shape=(
            jax.ShapeDtypeStruct((pieces, rows, spread), BF),
            jax.ShapeDtypeStruct((whole, rows, spread), BF),
            jax.ShapeDtypeStruct((whole, rows, spread), BF),
        ),
        grid_spec=pltpu.PrefetchScalarGridSpec(
            num_scalar_prefetch=2,
            grid=(end - first, pieces),
            in_specs=[
                own,
                own,
                own,
                pl.BlockSpec((1, count, rows), lambda g, i, b, o: ((g + first) * pieces + i, 0, 0)),
                every,
                every,
            ],
            out_specs=[own_out, every_out, every_out],
            scratch_shapes=[
                pltpu.VMEM((count, rows, min(128, lanes)), BF),
                pltpu.VMEM((count, rows, min(128, lanes)), BF),
                pltpu.VMEM((whole, lanes, rows), BF),
                pltpu.VMEM((count, head, rows), F32),
                pltpu.VMEM((whole, rows, lanes), F32),
                pltpu.VMEM((whole, rows, lanes), F32),
                pltpu.VMEM((count, rows), F32),
            ],
        ),
        compiler_params=pltpu.CompilerParams(vmem_limit_bytes=28 * MIB),
        cost_estimate=pl.CostEstimate(flops=25_000_000_000 * (end - first), bytes_accessed=10_000_000, transcendentals=0),
    )(*tables, queries, grad_rows, attended, totals, keys, values)


def xor_send(array, axis, bit):
    size = lax.axis_size(axis)
    return lax.ppermute(array, axis, [(i, i ^ bit) for i in range(size)])


def pick(array, index, axis=0):
    return lax.dynamic_index_in_dim(array, index, axis, keepdims=False)


def rows_at(array, index):
    return array.at[index].get(mode="promise_in_bounds")


def member_send(array, offset):
    if offset & 1:
        array = xor_send(array, "pb", 1)
    if offset >> 1:
        array = xor_send(array, "ka", offset >> 1)
    return array


def share_with_group(array, members):
    return jnp.concatenate([array] + [member_send(array, e) for e in range(1, members)], axis=0)


def plan_kernel(members, long, keys, me, held_piece, order, bounds, place, rank, by_rank, held):
    count = 4 * members

    def extremes(p, seen):
        return jnp.minimum(seen[0], keys[p]), jnp.maximum(seen[1], keys[p])

    least, most = lax.fori_loop(0, count, extremes, (keys[0], keys[0]))
    short = most - least >= long
    size = jnp.where(short, members // 2, members)

    def rank_one(p, _):
        r = lax.fori_loop(
            0, count, lambda q, r: r + jnp.where(keys[q] < keys[p], 1, 0), jnp.int32(0)
        )
        rank[p] = r
        by_rank[r] = p
        return 0

    lax.fori_loop(0, count, rank_one, 0)
    for e in range(members):
        member = me[0] ^ e
        second = jnp.where(short & (member >= members // 2), 1, 0)
        number = member - second * (members // 2)
        base = second * (2 * members)
        spread = (number, 2 * size - 1 - number, 2 * size + number, 4 * size - 1 - number)
        for i, r in enumerate(spread):
            held[4 * e + i] = base + r
            order[base + r] = 4 * e + i
            held_piece[4 * e + i] = by_rank[base + r]
            if e == 0:
                bounds[i] = base
                bounds[4 + i] = base + r

    def place_one(p, _):
        place[p] = order[rank[p]]
        return 0

    lax.fori_loop(0, count, place_one, 0)


def plan(keys, member, members, long):
    count = 4 * members
    smem = pl.BlockSpec(memory_space=pltpu.SMEM)
    table = jax.ShapeDtypeStruct((count,), jnp.int32)
    return pl.pallas_call(
        functools.partial(plan_kernel, members, long),
        out_shape=(table, table, jax.ShapeDtypeStruct((2 * OWN,), jnp.int32), table),
        in_specs=[smem, smem],
        out_specs=[smem] * 4,
        scratch_shapes=[pltpu.SMEM((count,), jnp.int32)] * 3,
    )(keys, jnp.reshape(member, (1,)).astype(jnp.int32))


class Layout:
    def __init__(self, sequence_ids, sequence_offsets):
        self.core = lax.axis_index("pb") % 2
        self.z = lax.axis_index("ka")
        self.depth = lax.axis_size("ka")
        self.subs = self.depth // 4
        self.members = self.depth // 2
        tall = sequence_ids.shape[0]
        self.rows = tall // OWN
        self.long = tall // BATCH * self.depth
        keys = (sequence_ids * self.long + sequence_offsets).reshape(OWN, self.rows)[:, :1]
        self.keys_under_way = self.send_in(
            jnp.broadcast_to(keys, (OWN, self.subs)).reshape(-1)
        )

    def settle(self):
        keys = self.arrived(self.keys_under_way).reshape(-1, self.subs)[:, 0]
        member = (self.z % self.subs) * 2 + self.core
        self.held_piece, self.order, self.bounds, self.place = plan(
            keys, member, self.members, self.long
        )
        self.tables = (self.bounds, self.order)

    def bits(self, place):
        return place // (2 * self.subs), place // self.subs % 2, place % self.subs

    def round_pairs(self, turn):
        pairs = []
        for pb in range(lax.axis_size("pb")):
            for z in range(self.depth):
                half, batch, sub = (a ^ b for a, b in zip(self.bits(z), self.bits(turn)))
                target = (2 * (pb % 2) + batch) * self.subs + sub
                pairs.append((pb * self.depth + z, (pb // 2 * 2 + half) * self.depth + target))
        return pairs

    def send_in(self, array):
        part_rows = array.shape[0] // (OWN * self.subs)
        blocks = array.reshape((BATCH, HALVES, self.subs, part_rows) + array.shape[1:])
        parts = []
        for turn in range(self.depth):
            half, batch, sub = (a ^ b for a, b in zip(self.bits(self.z), self.bits(turn)))
            part = pick(pick(pick(blocks, batch), half), sub)
            parts.append(lax.ppermute(part, ("pb", "ka"), self.round_pairs(turn)))
        return parts

    def arrived(self, parts):
        if self.subs == 1:
            return jnp.concatenate(parts + [xor_send(part, "pb", 1) for part in parts])
        held = jnp.concatenate(parts)
        part_rows, trailing = parts[0].shape[0], parts[0].shape[1:]
        held = held.reshape((4, self.subs, part_rows) + trailing)
        held = jnp.take(held, self.z % self.subs ^ jnp.arange(self.subs), axis=1)
        quarters = [[g * self.subs + i for i in range(self.subs)] for g in range(4)]
        held = lax.all_gather(held, "ka", axis=2, axis_index_groups=quarters)
        held = held.reshape((4 * self.subs * self.subs * part_rows,) + trailing)
        return jnp.concatenate([held, xor_send(held, "pb", 1)])


class Moving:
    def advance(self, value):
        self.launch(self.prepare(value))


class ScatterOut(Moving):
    def __init__(self, own, layout):
        self.layout = layout
        self.steps = ["first", "second", "assemble"]
        self.result = share_with_group(own, layout.members)

    def prepare(self, value):
        self.now = self.steps.pop(0) if self.steps else None
        turns = self.layout.depth // 2
        if self.now == "first":
            parts = self.parts(value)
            return parts[:turns], parts[turns:]
        return self.assemble(sum(value, [])) if self.now == "assemble" else value

    def launch(self, value):
        turns = self.layout.depth // 2
        if self.now == "first":
            value = (self.send(value[0], 0), value[1])
        elif self.now == "second":
            value = (value[0], self.send(value[1], turns))
        self.result = value

    def send(self, parts, first):
        return [
            lax.ppermute(part, ("pb", "ka"), [(b, a) for a, b in self.layout.round_pairs(turn)])
            for turn, part in enumerate(parts, first)
        ]

    def parts(self, shared):
        layout = self.layout
        subs = layout.subs
        rows, width = shared.shape[1:]
        shared = shared.reshape(-1, subs, rows // subs, width)
        sub = layout.z % subs
        parts = []
        for turn in range(layout.depth):
            piece = turn if subs == 1 else turn // subs * subs + (sub ^ turn % subs)
            parts.append(pick(pick(shared, pick(layout.place, piece)), sub))
        return parts

    def assemble(self, got):
        layout = self.layout
        subs = layout.subs
        order = []
        for block in range(OWN * subs):
            batch, half, part = block // (2 * subs), block // subs % 2, block % subs
            z_half, z_batch, z_sub = layout.bits(layout.z)
            order.append(((z_half ^ half) * 2 + (z_batch ^ batch)) * subs + (z_sub ^ part))
        return rows_at(jnp.stack(got), jnp.stack(order)).reshape(-1, got[0].shape[-1])


def stack_kernel(*refs):
    out, at = refs[-1], 0
    width = out.shape[1]
    for ref in refs[:-1]:
        for row in range(ref.shape[0]):
            for left in range(0, ref.shape[1], width):
                out[at : at + 1, :] = ref[row : row + 1, left : left + width]
                at += 1


def stack_rows(arrays):
    width = min(a.shape[1] for a in arrays)
    height = sum(a.size for a in arrays) // width
    vmem = pl.BlockSpec(memory_space=pltpu.VMEM)
    return pl.pallas_call(
        stack_kernel,
        out_shape=jax.ShapeDtypeStruct((height, width), F32),
        in_specs=[vmem] * len(arrays),
        out_specs=vmem,
        compiler_params=pltpu.CompilerParams(vmem_limit_bytes=4 * MIB),
    )(*arrays)


class VectorSum(Moving):
    def __init__(self, arrays):
        self.steps = []
        for axis in ("ka", "pb"):
            bits = lax.axis_size(axis).bit_length() - 1
            self.steps += [(axis, 1 << b) for b in range(bits)]
        self.result = stack_rows(arrays)

    def prepare(self, flat):
        self.now = self.steps.pop(0) if self.steps else None
        return flat

    def launch(self, flat):
        self.result = flat + xor_send(flat, *self.now) if self.now else flat


class BundleSum(Moving):
    def __init__(self, arrays, segments, at_once=False):
        self.along_pb, self.along_ka = lax.axis_size("pb"), lax.axis_size("ka")
        self.bits = self.along_pb.bit_length() - 1
        rest = list(range(1, self.bits))
        self.steps = ["core"] + list(zip(rest, rest[::-1]))
        self.steps += ["columns"] + list(range(1, self.along_ka.bit_length() - 1))
        self.narrow = arrays[0][0].shape[-1]
        self.segments = segments
        self.result = arrays
        if at_once:
            self.advance(arrays)

    def split(self, view, bit):
        axis = self.bits - 1 - bit
        own = (lax.axis_index("pb") >> bit) & 1
        kept = lax.dynamic_slice_in_dim(view, own, 1, axis)
        return kept, lax.dynamic_slice_in_dim(view, 1 - own, 1, axis)

    def prepare(self, views):
        self.now = step = self.steps.pop(0) if self.steps else None
        if step is None or step == "core":
            return views
        if isinstance(step, tuple):
            if len(views) == 1:
                half = views[0].shape[-2] // 2
                views = [views[0][..., :half, :], views[0][..., half:, :]]
            return [self.split(view, bit) for view, bit in zip(views, step)]
        if step == "columns":
            return split_columns(
                [v.reshape(-1, self.narrow) for v in views], self.segments, self.along_ka
            )
        own = (lax.axis_index("ka") >> step) & 1
        pairs = views.reshape((-1, 2) + views.shape[1:])
        return pick(pairs, own, 1), pick(pairs, 1 - own, 1)

    def launch(self, made):
        step = self.now
        if step is None:
            self.result = made
        elif step == "core":
            shape = (2,) * (self.bits - 1) + (1,)
            self.result = [
                (kept + xor_send(sent, "pb", 1)).reshape(shape + kept.shape[1:])
                for kept, sent in made
            ]
        elif isinstance(step, tuple):
            self.result = [
                kept + xor_send(sent, "pb", 1 << bit) for (kept, sent), bit in zip(made, step)
            ]
        else:
            kept, sent = made
            got = xor_send(sent, "ka", 1 if step == "columns" else 1 << step)
            self.result = kept + got if self.steps else [kept[0], got[0]]

    def matrices(self):
        return join_columns(self.result, self.segments, self.narrow, self.along_ka)


def split_kernel(segments, ways, z, *refs):
    views, (kept, sent, whole) = refs[:-3], refs[-3:]
    at = 0
    for view in views:
        whole[at : at + view.shape[0], :] = view[...]
        at += view.shape[0]
    narrow = whole.shape[1]
    thin = narrow // ways
    for target in range(ways):
        pieces, at = [], 0
        for height, folds in segments:
            share = ways // folds
            first = at + target // share * height
            wide = narrow // share
            for i in range(wide // thin):
                left = target % share * wide + i * thin
                pieces.append(whole[first : first + height, left : left + thin])
            at += height * folds
        rows = jnp.concatenate(pieces, axis=0)
        half = rows.shape[0] // 2
        block = jnp.concatenate([rows[:half], rows[half:]], axis=1)
        mine = z[0] % 2 == target % 2

        @pl.when(mine)
        def _():
            kept[target // 2] = block

        @pl.when(jnp.logical_not(mine))
        def _():
            sent[target // 2] = block


def split_columns(views, segments, ways):
    narrow = views[0].shape[1]
    height = sum(v.shape[0] for v in views)
    shape = jax.ShapeDtypeStruct((ways // 2, height // 2, 2 * narrow // ways), BF)
    vmem = pl.BlockSpec(memory_space=pltpu.VMEM)
    return pl.pallas_call(
        functools.partial(split_kernel, segments, ways),
        out_shape=[shape] * 2,
        in_specs=[pl.BlockSpec(memory_space=pltpu.SMEM)] + [vmem] * len(views),
        out_specs=[vmem] * 2,
        scratch_shapes=[pltpu.VMEM((height, narrow), BF)],
        compiler_params=pltpu.CompilerParams(vmem_limit_bytes=16 * MIB),
    )(lax.axis_index("ka").reshape(1).astype(jnp.int32), *views)


def join_kernel(segments, narrow, ways, *refs):
    outs = refs[2:]
    total = refs[0][...].astype(F32) + refs[1][...].astype(F32)
    thin = narrow // ways
    rows = jnp.concatenate([total[:, :thin], total[:, thin:]], axis=0)
    at = 0
    for (height, folds), out in zip(segments, outs):
        pieces = [rows[at + i * height : at + (i + 1) * height] for i in range(folds)]
        out[...] = pieces[0] if folds == 1 else jnp.concatenate(pieces, axis=1)
        at += height * folds


def join_columns(parts, segments, narrow, ways):
    vmem = pl.BlockSpec(memory_space=pltpu.VMEM)
    thin = narrow // ways
    return pl.pallas_call(
        functools.partial(join_kernel, segments, narrow, ways),
        out_shape=[jax.ShapeDtypeStruct((height, thin * folds), F32) for height, folds in segments],
        in_specs=[vmem] * 2,
        out_specs=[vmem] * len(segments),
        compiler_params=pltpu.CompilerParams(vmem_limit_bytes=16 * MIB),
    )(*parts)


class Background:
    def __init__(self):
        self.moving = []

    def tick(self, value):
        live = [m for m in self.moving if not getattr(m, "ended", False)]
        value, results = lax.optimization_barrier((value, [m.result for m in live]))
        for m in live:
            m.ended = not m.steps
        made = [m.prepare(r) for m, r in zip(live, results)]
        value, made = lax.optimization_barrier((value, made))
        for m, parts in zip(live, made):
            m.launch(parts)
        return value

    def drain(self):
        for m in self.moving:
            while m.steps:
                m.advance(m.result)


def normalized(values):
    centre = values - jnp.mean(values, axis=-1, keepdims=True)
    spread = jnp.mean(centre * centre, axis=-1, keepdims=True)
    scale = lax.rsqrt(spread + EPSILON)
    return centre * scale, scale


def layer_norm(values, gain, shift):
    return (normalized(values)[0] * gain.astype(F32) + shift.astype(F32)).astype(BF)


def norm_backward(values, gain, upstream):
    n, scale = normalized(values)
    vectors = jnp.sum(jnp.stack([upstream * n, upstream]), axis=1)
    dn = upstream * gain.astype(F32)
    mean = jnp.mean(dn, axis=-1, keepdims=True)
    along = jnp.mean(dn * n, axis=-1, keepdims=True)
    return scale * (dn - mean - n * along), vectors


def gelu_pair(u):
    size = jnp.abs(u) * 0.7071067811865476
    t = 1.0 / (1.0 + 0.3275911 * size)
    bell = jnp.exp(-0.5 * u * u)
    series = t * (
        0.254829592
        + t * (-0.284496736 + t * (1.421413741 + t * (-1.453152027 + t * 1.061405429)))
    )
    tail = 0.5 * series * bell
    phi = jnp.where(u < 0, tail, 1.0 - tail)
    return u * phi, phi + u * (bell * 0.3989422804014327)


def row_tiles(tall):
    tile = min(256, tall)
    return [slice(r, r + tile) for r in range(0, tall, tile)]


def norm_rows(values, gain, shift):
    centre = values - jnp.mean(values, axis=-1, keepdims=True)
    spread = jnp.mean(centre * centre, axis=-1, keepdims=True)
    return (centre * lax.rsqrt(spread + EPSILON) * gain + shift).astype(BF)


def mlp_kernel(
    following, o_ref, x_ref, wo_ref, gain_ref, bias_ref, wu_ref, ub_ref, wd_ref, db_ref, ng_ref, nb_ref,
    x1_ref, h2_ref, a_ref, s_ref, y_ref, *rest,
):
    acc = rest[-1]
    step = pl.program_id(0)
    tiles = row_tiles(o_ref.shape[0])

    @pl.when(step == 0)
    def _():
        gain, shift = gain_ref[...].astype(F32), bias_ref[...].astype(F32)
        for t in tiles:
            x1 = x_ref[t].astype(F32) + dot(o_ref[t], wo_ref[...])
            x1_ref[t] = x1
            h2_ref[t] = norm_rows(x1, gain, shift)
            acc[t] = jnp.zeros_like(x1)

    up_bias = ub_ref[...].astype(F32)
    hidden = [dot(h2_ref[t], wu_ref[...]) for t in tiles]
    actives = []
    for t, u in zip(tiles, hidden):
        active, slope = gelu_pair(u + up_bias)
        actives.append(active.astype(BF))
        a_ref[t] = actives[-1]
        s_ref[t] = slope.astype(BF)
    for t, active in zip(tiles, actives):
        acc[t] += dot(active, wd_ref[...])

    @pl.when(step == pl.num_programs(0) - 1)
    def _():
        down_bias = db_ref[...].astype(F32)
        gain, shift = ng_ref[...].astype(F32), nb_ref[...].astype(F32)
        for t in tiles:
            y = x1_ref[t] + (acc[t] + down_bias)
            y_ref[t] = y.astype(y_ref.dtype)
            if following:
                rest[0][t] = norm_rows(y, gain, shift)


ONCE = pl.Buffered(1)


def whole_block(array):
    return pl.BlockSpec(array.shape, lambda i: (0,) * len(array.shape), pipeline_mode=ONCE)


def cost(flops, *arrays):
    moved = sum(a.size * a.dtype.itemsize for a in arrays)
    return pl.CostEstimate(flops=flops, bytes_accessed=moved, transcendentals=0)


def mlp_forward(attended, x_own, params, following):
    (_, _, _, _, _, w_out, mlp_gain, mlp_bias, w_up, up_bias, w_down, down_bias) = params
    tall, width = attended.shape
    hidden = w_up.shape[1]
    row = lambda v: v.reshape(1, -1)
    gain, shift = following or (mlp_gain, mlp_bias)
    inputs = (
        attended, x_own, w_out, row(mlp_gain), row(mlp_bias), w_up, row(up_bias), w_down,
        row(down_bias), row(gain), row(shift),
    )
    specs = [whole_block(a) for a in inputs]
    specs[5] = pl.BlockSpec((width, width), lambda i: (0, i))
    specs[6] = pl.BlockSpec((1, width), lambda i: (0, i))
    specs[7] = pl.BlockSpec((width, width), lambda i: (i, 0))
    wide, narrow = (tall, hidden), (tall, width)
    shapes = [(narrow, F32), (narrow, BF), (wide, BF), (wide, BF), (narrow, F32 if following else BF)]
    shapes += [(narrow, BF)] if following else []
    out_shape = [jax.ShapeDtypeStruct(shape, kind) for shape, kind in shapes]
    chunk = pl.BlockSpec((tall, width), lambda i: (0, i))
    full = pl.BlockSpec((tall, width), lambda i: (0, 0), pipeline_mode=ONCE)
    return pl.pallas_call(
        functools.partial(mlp_kernel, following is not None),
        out_shape=out_shape,
        grid=(hidden // width,),
        in_specs=specs,
        out_specs=[full, full, chunk, chunk, full] + ([full] if following else []),
        scratch_shapes=[pltpu.VMEM((tall, width), F32)],
        compiler_params=pltpu.CompilerParams(vmem_limit_bytes=36 * MIB),
        cost_estimate=cost(2 * tall * width * (2 * hidden + width), *inputs, *out_shape),
    )(*inputs)


def mlp_back_kernel(
    g_ref, slope_ref, wd_ref, wu_ref, x1_ref, gain_ref, wo_ref,
    du_ref, dx_ref, gx_ref, do_ref, gb_ref, sums_ref, vectors_ref, acc,
):
    step = pl.program_id(0)
    tiles = row_tiles(g_ref.shape[0])

    @pl.when(step == 0)
    def _():
        for t in tiles:
            gb_ref[t] = g_ref[t].astype(BF)
            acc[t] = jnp.zeros(acc[t].shape, F32)

    total = 0.0
    products = [dot(gb_ref[t], wd_ref[...], NT) for t in tiles]
    for t, da in zip(tiles, products):
        du = (da * slope_ref[t].astype(F32)).astype(BF)
        du_ref[t] = du
        total = total + jnp.sum(du.astype(F32), axis=0, keepdims=True)
        acc[t] += dot(du, wu_ref[...], NT)
    sums_ref[...] = total

    @pl.when(step == pl.num_programs(0) - 1)
    def _():
        gain = gain_ref[...].astype(F32)
        of_gain = of_shift = of_down = 0.0
        for t in tiles:
            dh2, x1 = acc[t], x1_ref[t]
            centre = x1 - jnp.mean(x1, axis=-1, keepdims=True)
            scale = lax.rsqrt(jnp.mean(centre * centre, axis=-1, keepdims=True) + EPSILON)
            n = centre * scale
            of_gain = of_gain + jnp.sum(dh2 * n, axis=0, keepdims=True)
            of_shift = of_shift + jnp.sum(dh2, axis=0, keepdims=True)
            of_down = of_down + jnp.sum(gb_ref[t].astype(F32), axis=0, keepdims=True)
            dn = dh2 * gain
            mean = jnp.mean(dn, axis=-1, keepdims=True)
            along = jnp.mean(dn * n, axis=-1, keepdims=True)
            dx = g_ref[t].astype(F32) + scale * (dn - mean - n * along)
            dx_ref[t] = dx
            gx = dx.astype(BF)
            gx_ref[t] = gx
            do_ref[t] = dot(gx, wo_ref[...], NT).astype(BF)
        vectors_ref[0:1, :] = of_gain
        vectors_ref[1:2, :] = of_shift
        vectors_ref[2:3, :] = of_down


def mlp_backward(upstream, slope, middle, params):
    (_, _, _, _, _, w_out, mlp_gain, _, w_up, _, w_down, _) = params
    tall, width = upstream.shape
    hidden = slope.shape[1]
    inputs = (upstream, slope, w_down, w_up, middle, mlp_gain.reshape(1, -1), w_out)
    specs = [whole_block(a) for a in inputs]
    specs[1] = pl.BlockSpec((tall, width), lambda i: (0, i))
    specs[2] = pl.BlockSpec((width, width), lambda i: (i, 0))
    specs[3] = pl.BlockSpec((width, width), lambda i: (0, i))
    shapes = [((tall, hidden), BF), ((tall, width), F32)] + [((tall, width), BF)] * 3
    shapes += [((1, hidden), F32), ((3, width), F32)]
    out_shape = [jax.ShapeDtypeStruct(shape, kind) for shape, kind in shapes]
    full = pl.BlockSpec((tall, width), lambda i: (0, 0), pipeline_mode=ONCE)
    return pl.pallas_call(
        mlp_back_kernel,
        out_shape=out_shape,
        grid=(hidden // width,),
        in_specs=specs,
        out_specs=[
            pl.BlockSpec((tall, width), lambda i: (0, i)), full, full, full, full,
            pl.BlockSpec((1, width), lambda i: (0, i)), pl.BlockSpec((3, width), lambda i: (0, 0)),
        ],
        scratch_shapes=[pltpu.VMEM((tall, width), F32)],
        compiler_params=pltpu.CompilerParams(vmem_limit_bytes=40 * MIB),
        cost_estimate=cost(2 * tall * width * (2 * hidden + width), *inputs, *out_shape),
    )(*inputs)


def put_halves(core, kept_ref, sent_ref, low, high):
    @pl.when(core == 0)
    def _():
        kept_ref[...] = low
        sent_ref[...] = high

    @pl.when(core != 0)
    def _():
        kept_ref[...] = high
        sent_ref[...] = low


def by_blocks(product, blocks):
    height, breadth = product.shape
    parts = product.astype(BF).reshape(blocks // 2, 2, height // blocks, breadth)
    return parts[:, 0], parts[:, 1]


def mlp_weights_kernel(
    blocks, folds, core, h2_ref, du_ref, o_ref, gx_ref, a_ref, gb_ref,
    kept_a, sent_a, kept_b, sent_b,
):
    step = pl.program_id(0)

    @pl.when(step < folds)
    def _():
        put_halves(core[0], kept_a, sent_a, *by_blocks(dot(h2_ref[...], du_ref[...], TN), blocks))

    @pl.when(step == folds)
    def _():
        put_halves(core[0], kept_a, sent_a, *by_blocks(dot(o_ref[...], gx_ref[...], TN), blocks))

    @pl.when(step > folds)
    def _():
        product = dot(a_ref[...], gb_ref[...], TN)
        pairs, _, height, _ = kept_b.shape
        parts = product.astype(BF).reshape(pairs, 1, 2, height, product.shape[1])
        put_halves(core[0], kept_b, sent_b, parts[:, :, 0], parts[:, :, 1])


def mlp_weights(h2, du, attended, gx, active, gb):
    blocks = lax.axis_size("pb")
    tall, width = h2.shape
    hidden = du.shape[1]
    folds = hidden // width
    thin, tall_block = width // blocks, hidden // blocks
    pairs = blocks // 2 // folds
    full = pl.BlockSpec((tall, width), lambda i, c: (0, 0), pipeline_mode=ONCE)
    a_block = pl.BlockSpec(
        (blocks // 2, thin, width), lambda i, c: (0, jnp.minimum(i, folds), 0)
    )
    b_block = pl.BlockSpec(
        (pairs, 1, tall_block, width), lambda i, c: (jnp.maximum(i - folds - 1, 0), 0, 0, 0)
    )
    a_shape = jax.ShapeDtypeStruct((blocks // 2, thin * (folds + 1), width), BF)
    b_shape = jax.ShapeDtypeStruct((blocks // 2, 1, tall_block, width), BF)
    core = (lax.axis_index("pb") % 2).reshape(1).astype(jnp.int32)
    inputs = (h2, du, attended, gx, active, gb)
    kept_a, sent_a, kept_b, sent_b = pl.pallas_call(
        functools.partial(mlp_weights_kernel, blocks, folds),
        out_shape=(a_shape, a_shape, b_shape, b_shape),
        grid_spec=pltpu.PrefetchScalarGridSpec(
            num_scalar_prefetch=1,
            grid=(2 * folds + 1,),
            in_specs=[
                full,
                pl.BlockSpec((tall, width), lambda i, c: (0, jnp.minimum(i, folds - 1))),
                full,
                full,
                pl.BlockSpec((tall, width), lambda i, c: (0, jnp.clip(i - folds - 1, 0, folds - 1))),
                full,
            ],
            out_specs=[a_block, a_block, b_block, b_block],
        ),
        compiler_params=pltpu.CompilerParams(vmem_limit_bytes=32 * MIB),
        cost_estimate=cost(2 * tall * width * (2 * hidden + width), *inputs, a_shape, b_shape),
    )(core, *inputs)
    flat = lambda v: v.reshape(blocks // 2, tall_block, width)
    arrays = [(kept_a, sent_a), (flat(kept_b), flat(sent_b))]
    return BundleSum(arrays, [(thin, folds), (thin, 1), (tall_block, 1)])


def attention_weights_kernel(blocks, core, *refs):
    h_ref, kept_ref, sent_ref = refs[0], refs[-2], refs[-1]
    parts = refs[1:-2]
    count = len(parts) // 3
    for which in range(3):

        @pl.when(pl.program_id(0) == which)
        def _():
            products = [
                dot(h_ref[: part.shape[0], :], part[...], TN)
                for part in parts[which * count : (which + 1) * count]
            ]
            product = products[0] if count == 1 else jnp.concatenate(products, axis=1)
            put_halves(core[0], kept_ref, sent_ref, *by_blocks(product, blocks))


def attention_weights(h_all, dqs, dks, dvs):
    blocks = lax.axis_size("pb")
    width = h_all.shape[1]
    thin = width // blocks
    inputs = (h_all, *dqs, *dks, *dvs)
    block = pl.BlockSpec((blocks // 2, thin, width), lambda i, c: (0, i, 0))
    shape = jax.ShapeDtypeStruct((blocks // 2, 3 * thin, width), BF)
    core = (lax.axis_index("pb") % 2).reshape(1).astype(jnp.int32)
    kept, sent = pl.pallas_call(
        functools.partial(attention_weights_kernel, blocks),
        out_shape=(shape, shape),
        grid_spec=pltpu.PrefetchScalarGridSpec(
            num_scalar_prefetch=1,
            grid=(3,),
            in_specs=[
                pl.BlockSpec(a.shape, lambda i, c: (0, 0), pipeline_mode=ONCE) for a in inputs
            ],
            out_specs=[block, block],
        ),
        compiler_params=pltpu.CompilerParams(vmem_limit_bytes=28 * MIB),
        cost_estimate=cost(5 * h_all.shape[0] * width * width, *inputs, shape),
    )(core, *inputs)
    return BundleSum([(kept, sent)], [(thin, 1)] * 3, at_once=True)


def layer_forward(x_own, h_all, params, layout, signed, passing, following):
    (_, _, w_query, w_key, w_value, *_) = params
    tall, width = x_own.shape
    rows = layout.rows
    scale = (width // HEADS) ** -0.5
    queries = (dense(h_all[:tall], w_query, 1, 0) * scale).astype(BF).reshape(OWN, rows, width)
    keys = dense(h_all, w_key, 1, 0).astype(BF).reshape(-1, rows, width)
    values = dense(h_all, w_value, 1, 0).astype(BF).reshape(-1, rows, width)
    attended, totals = attend_forward(queries, keys, values, layout.tables, signed)
    (attended, totals), passing = lax.optimization_barrier(((attended, totals), passing))
    middle, h2, active, slope, *result = mlp_forward(
        attended.reshape(tall, width), x_own, params, following
    )
    saved = (h_all, queries, keys, values, attended, totals, middle, h2, active, slope)
    return result, saved, passing


def layer_backward(upstream, x_own, params, saved, layout, signed, background, cuts, earlier):
    (norm_gain, _, w_query, w_key, w_value, *_) = params
    h_all, queries, keys, values, attended, totals, middle, h2, active, slope = saved
    tall, width = x_own.shape
    du, dx1, gx, do, gb, sum_du, vectors = mlp_backward(upstream, slope, middle, params)
    mlp_vectors = [vectors, sum_du]
    if earlier:
        du, gx, do, gb = background.tick((du, gx, do, gb))
    sum_mlp = mlp_weights(h2, du, attended.reshape(tall, width), gx, active, gb)
    background.moving.append(sum_mlp)
    sum_vectors = VectorSum(earlier + mlp_vectors) if earlier else None
    if earlier:
        background.moving.append(sum_vectors)
    do = do.reshape(queries.shape)
    outcome = []
    for first, end in zip(cuts, cuts[1:]):
        do = background.tick(do)
        if end > first:
            outcome.append(
                attend_backward(
                    queries, do, attended, totals, keys, values, layout.tables, signed, first, end
                )
            )
            do, outcome[-1] = lax.optimization_barrier((do, outcome[-1]))
    outcome = background.tick(outcome)
    dqs, dks, dvs = ([p.reshape(-1, p.shape[-1]) for p in parts] for parts in zip(*outcome))
    dq, dk, dv = (jnp.concatenate(parts, axis=-1) for parts in (dqs, dks, dvs))
    from_keys = (dense(dk, w_key, 1, 1) + dense(dv, w_value, 1, 1)).astype(BF)
    (dqs, dks, dvs), from_keys = lax.optimization_barrier(((dqs, dks, dvs), from_keys))
    from_keys = from_keys.reshape(layout.members, tall, width)
    given = [member_send(from_keys[e], e) for e in range(1, layout.members)]
    dh = dense(dq, w_query, 1, 1) + from_keys[0].astype(F32)
    sum_att = attention_weights(h_all, dqs, dks, dvs)
    background.moving.append(sum_att)
    for part in given:
        dh = dh + part.astype(F32)
    dx, norm_vectors = norm_backward(x_own.astype(F32), norm_gain, dh)

    def finish(mlp, norm):
        up, out, down = sum_mlp.matrices()
        query, key, value = sum_att.matrices()
        return (
            norm[0], norm[1], query, key, value, out,
            mlp[0], mlp[1], up, mlp[3:].reshape(-1), down, mlp[2],
        )

    return dx1 + dx, mlp_vectors, norm_vectors, sum_vectors, finish


def per_device(tokens, sequence_ids, sequence_offsets, *rest):
    signed_params, plain_params, cotangent = rest[:12], rest[12:24], rest[24]
    tall, width = tokens.shape
    layout = Layout(sequence_ids, sequence_offsets)
    tokens, layout.keys_under_way = lax.optimization_barrier((tokens, layout.keys_under_way))
    rows = layout.rows
    background = Background()
    x_all = layout.arrived(layout.send_in(tokens)).reshape(-1, rows, width)
    layout.settle()
    x_held = rows_at(x_all, layout.held_piece).reshape(-1, width)
    cotangent, x_held = lax.optimization_barrier((cotangent, x_held))
    cotangent = layout.send_in(cotangent)
    h_all = layer_norm(x_held.astype(F32), signed_params[0], signed_params[1])
    x_own = x_held[:tall]
    (between, h_own), signed_saved, cotangent = layer_forward(
        x_own, h_all, signed_params, layout, True, cotangent, plain_params[:2]
    )
    h_all = share_with_group(h_own, layout.members)
    upstream = layout.arrived(cotangent).reshape(-1, rows, width)
    (final,), plain_saved, upstream = layer_forward(
        between, h_all, plain_params, layout, False, upstream, None
    )
    output = ScatterOut(final.reshape(OWN, rows, width), layout)
    background.moving.append(output)
    upstream = rows_at(upstream, layout.held_piece[:OWN]).reshape(tall, width)
    groups = attention_sizes(width)[2]
    upstream, mlp_plain, norm_plain, _, finish_plain = layer_backward(
        upstream, between, plain_params, plain_saved, layout, False, background,
        (0, groups // 3, groups), [],
    )
    upstream = background.tick(upstream)
    upstream, _, norm_signed, early, finish_signed = layer_backward(
        upstream, x_own, signed_params, signed_saved, layout, True, background,
        tuple(range(groups + 1)), mlp_plain + [norm_plain],
    )
    upstream = background.tick(upstream)
    back = ScatterOut(upstream.astype(BF).reshape(OWN, rows, width), layout)
    late = VectorSum([norm_signed])
    for _ in range(2):
        late.advance(late.result)
    background.moving += [back, late]
    background.tick(())
    background.tick(())
    background.drain()
    count = signed_params[8].shape[1] // width + 3
    early, late = early.result, late.result
    return (
        (output.result, back.result.astype(F32))
        + finish_signed(early[count + 2 :], late)
        + finish_plain(early[:count], early[count : count + 2])
    )


def solution(mesh):
    rows, block = P(("pb", "ka"), None), P("pb", "ka")
    grads = (P(), P(), block, block, block, block, P(), P(), block, P(), block, P())
    return jax.shard_map(
        per_device,
        mesh=mesh,
        in_specs=(rows, P(("pb", "ka")), P(("pb", "ka"))) + (P(),) * 24 + (rows,),
        out_specs=(rows, rows) + grads + grads,
        check_vma=False,
    )
```
